32 devices in a mesh: frame: 4 (over z), tile: 8 (over y, x, core).
Axes of the slice: x: 2, y: 2, z: 4, core: 2. Of those that a mesh axis runs over, the one named last changes fastest.
Arguments:
- displacement: bfloat16 [512, 2, 8, 4096], P('frame', None, 'tile'), may hold values from -256 to 256
Outputs:
- basis: bfloat16 [512, 3, 8, 4096], P(None, None, 'tile', 'frame')
- factor: float32 [512, 512], replicated
The draws below stay inside these ranges and needn't reach their ends.
All inputs are finite; a program needn't handle non-finite values.
Results may differ from the reference program's by a relative error of at most 0.0053.
The reference program's roundings to bfloat16 on the way (of `strain`) count: a program that leaves them out, or rounds other values in their place, can miss the bound.
Values may be sent and summed in bfloat16 or wider, within the bound.
A program may use at most 64 MiB of HBM per device.

```python
import math
import jax
import jax.numpy as jnp
from jax import lax

F = 512
W = 4096
H = 8


def draw_displacement(key, part):
    keys = jax.random.split(jax.random.fold_in(key, 11), 4)
    noise = jax.random.truncated_normal(keys[0], -4.0, 4.0, (F, 2, H, W), jnp.float32)
    scales = jnp.exp(jax.random.uniform(keys[1], (F,), jnp.float32, math.log(0.5), math.log(2.0)))
    weight = 0.3
    modes = jax.random.truncated_normal(keys[2], -4.0, 4.0, (4, 2, H, W), jnp.float32)
    coeffs = jax.random.truncated_normal(keys[3], -3.0, 3.0, (F, 4), jnp.float32)
    field = noise
    for index in range(4):
        field = field + weight * coeffs[:, index][:, None, None, None] * modes[index][None]
    ramp_rows = 1.0 + (math.sqrt(3.0) - 1.0) * jnp.arange(H, dtype=jnp.float32) / max(H - 1, 1)
    ramp_cols = 1.0 + (math.sqrt(3.0) - 1.0) * jnp.arange(W, dtype=jnp.float32) / max(W - 1, 1)
    return (scales[:, None, None, None] * field * ramp_rows[None, None, :, None] * ramp_cols[None, None, None, :]).astype(jnp.bfloat16)


def setup_inputs(seed: int = 0) -> dict:
    seeds = jax.random.split(jax.random.key(seed), 2)
    return {
        "displacement": draw_displacement(jax.random.fold_in(seeds[1], 71), 0),
    }


def derivative(center, before, after, first, final):
    return jnp.where(first, after - center, jnp.where(final, center - before, (after - before) * 0.5))

def column_derivative(center):
    width = center.shape[-1]
    after = jnp.concatenate([center[..., 1:], center[..., -1:]], axis=-1)
    before = jnp.concatenate([center[..., :1], center[..., :-1]], axis=-1)
    column = jnp.arange(width, dtype=jnp.int32)
    return derivative(center, before, after, column == 0, column == width - 1)

def strain_row(displacement, row):
    height = displacement.shape[2]
    above_row = jnp.maximum(row - 1, 0).astype(jnp.int32)
    below_row = jnp.minimum(row + 1, height - 1).astype(jnp.int32)
    center = lax.dynamic_index_in_dim(displacement, row, 2, keepdims=False).astype(jnp.float32)
    above = lax.dynamic_index_in_dim(displacement, above_row, 2, keepdims=False).astype(jnp.float32)
    below = lax.dynamic_index_in_dim(displacement, below_row, 2, keepdims=False).astype(jnp.float32)
    d_rows = derivative(center, above, below, row == 0, row == height - 1)
    d_cols = column_derivative(center)
    strain = jnp.stack([d_cols[:, 0], d_rows[:, 1], 0.5 * (d_rows[:, 0] + d_cols[:, 1])], axis=1)
    return strain.astype(jnp.bfloat16)

def reference(displacement):
    frames = displacement.shape[0]
    height = displacement.shape[2]
    width = displacement.shape[3]
    scale = math.sqrt(3 * height * width)

    def accumulate(gram, row):
        strain = strain_row(displacement, row)
        flat = strain.reshape(frames, 3 * width)
        gram = gram + lax.dot_general(flat.astype(jnp.float32), flat.astype(jnp.float32), (((1,), (1,)), ((), ())), preferred_element_type=jnp.float32)
        return (gram, strain)
    gram, strains = lax.scan(accumulate, jnp.zeros((frames, frames), jnp.float32), jnp.arange(height, dtype=jnp.int32))
    lower = jnp.linalg.cholesky(gram)

    def solve(strain):
        flat = strain.reshape(frames, 3 * width).astype(jnp.float32)
        solved = lax.linalg.triangular_solve(lower, flat, left_side=True, lower=True)
        return (solved * scale).astype(jnp.bfloat16)
    basis_rows = lax.map(solve, strains)
    basis = jnp.transpose(basis_rows.reshape(height, frames, 3, width), (1, 2, 0, 3))
    return (basis, lower.T / scale)
```

```python
import functools
import math

import jax
import jax.numpy as jnp
from jax import lax
from jax.experimental import pallas as pl
from jax.experimental.pallas import tpu as pltpu
from jax.sharding import PartitionSpec as P

MESH = pl.DeviceIdType.MESH
BLOCK = 128
NT = (((1,), (1,)), ((), ()))
TN = (((0,), (0,)), ((), ()))
EXACT = lax.Precision.HIGHEST


def sum_stages(nz, nt, rows):
    stages = []
    for axis, peers in (("tile", nt), ("frame", nz)):
        distance = 1
        while distance < peers:
            halved = rows % 16 == 0
            rows = rows // 2 if halved else rows
            stages.append((axis, distance, rows, halved))
            distance *= 2
    return stages


def exchange_kernel(nz, nt, stages, x_ref, gram_ref, s_ref, center, above, below, edge_out, edge_in,
                    edge_cols, acc, landing, total, own_sem, a2a_send, a2a_recv, edge_send, edge_recv,
                    up_send, up_recv, dn_send, dn_recv, sum_send, sum_recv):
    z, t = lax.axis_index("frame"), lax.axis_index("tile")
    fb, wb = x_ref.shape[1], x_ref.shape[2] // nz
    frames = fb * nz

    barrier = pltpu.get_barrier_semaphore()
    greeted = 0
    for k in range(1, nz):
        pl.semaphore_signal(barrier, inc=1, device_id={"frame": lax.rem(z + k, nz)}, device_id_type=MESH)
        greeted += 1
    for k in (1, nt - 1):
        pl.semaphore_signal(barrier, inc=1, device_id={"tile": lax.rem(t + k, nt)}, device_id_type=MESH)
        greeted += 1
    distance = 2
    while distance < nt:
        peer = t + distance * (1 - 2 * ((t // distance) % 2))
        pl.semaphore_signal(barrier, inc=1, device_id={"tile": peer}, device_id_type=MESH)
        greeted += 1
        distance *= 2
    pl.semaphore_wait(barrier, greeted)

    own = pltpu.make_async_copy(
        x_ref.at[:, :, pl.ds(pl.multiple_of(z * wb, 128), wb)],
        center.at[:, pl.ds(pl.multiple_of(z * fb, 16), fb), :], own_sem)
    own.start()
    blocks = [None]
    for k in range(1, nz):
        d = lax.rem(z + k, nz)
        copy = pltpu.make_async_remote_copy(
            src_ref=x_ref.at[:, :, pl.ds(pl.multiple_of(d * wb, 128), wb)],
            dst_ref=center.at[:, pl.ds(pl.multiple_of(z * fb, 16), fb), :],
            send_sem=a2a_send.at[k], recv_sem=a2a_recv.at[k],
            device_id={"frame": d}, device_id_type=MESH)
        copy.start()
        blocks.append(copy)

    row16 = lax.broadcasted_iota(jnp.int32, (16, 128), 0)
    lane16 = lax.broadcasted_iota(jnp.int32, (16, 128), 1)

    def pick(row, lane):
        return jnp.where((row16 == row) & (lane16 == lane), 1.0, 0.0).astype(jnp.bfloat16)

    for d in range(nz):
        total_edge = jnp.zeros((16, fb), jnp.float32)
        for c in range(2):
            if d > 0:
                total_edge += lax.dot_general(pick(2 * c, 127), x_ref[c, :, d * wb - 128:d * wb], NT,
                                              preferred_element_type=jnp.float32)
            if d < nz - 1:
                total_edge += lax.dot_general(pick(2 * c + 1, 0), x_ref[c, :, (d + 1) * wb:(d + 1) * wb + 128], NT,
                                              preferred_element_type=jnp.float32)
        edge_out[d] = total_edge.astype(jnp.bfloat16)
    edges = [None]
    for k in range(1, nz):
        d = lax.rem(z + k, nz)
        copy = pltpu.make_async_remote_copy(
            src_ref=edge_out.at[d], dst_ref=edge_in.at[z],
            send_sem=edge_send.at[k], recv_sem=edge_recv.at[k],
            device_id={"frame": d}, device_id_type=MESH)
        copy.start()
        edges.append(copy)
    edge_in[z] = edge_out[z]

    halos = []
    for k in range(nz):
        if k == 0:
            own.wait()
        else:
            blocks[k].wait_recv()
        s = lax.rem(z - k + nz, nz)
        rows = pl.ds(pl.multiple_of(s * fb, 16), fb)
        up = pltpu.make_async_remote_copy(
            src_ref=center.at[:, rows, :], dst_ref=above.at[:, rows, :],
            send_sem=up_send.at[k], recv_sem=up_recv.at[k],
            device_id={"tile": lax.rem(t + 1, nt)}, device_id_type=MESH)
        dn = pltpu.make_async_remote_copy(
            src_ref=center.at[:, rows, :], dst_ref=below.at[:, rows, :],
            send_sem=dn_send.at[k], recv_sem=dn_recv.at[k],
            device_id={"tile": lax.rem(t + nt - 1, nt)}, device_id_type=MESH)
        halos.append((up, dn, s))

        @pl.when(t < nt - 1)
        def _(up=up):
            up.start()

        @pl.when(t > 0)
        def _(dn=dn):
            dn.start()

    lane = lax.broadcasted_iota(jnp.int32, (16, wb), 1)
    outer_first, outer_last = (z == 0), (z == nz - 1)
    at_first, at_last = lane == 0, lane == wb - 1
    col_scale = jnp.where((at_first & outer_first) | (at_last & outer_last), 1.0, 0.5)
    row_scale = jnp.where((t == 0) | (t == nt - 1), 1.0, 0.5)
    eye = jnp.where(row16 == lane16, 1.0, 0.0).astype(jnp.bfloat16)

    for k in range(nz):
        up, dn, s = halos[k]
        base = s * fb

        @pl.when(t > 0)
        def _(up=up):
            up.wait_recv()

        @pl.when(t < nt - 1)
        def _(dn=dn):
            dn.wait_recv()

        rows = pl.ds(pl.multiple_of(base, 16), fb)

        @pl.when(t == 0)
        def _(rows=rows):
            above[:, rows, :] = center[:, rows, :]

        @pl.when(t == nt - 1)
        def _(rows=rows):
            below[:, rows, :] = center[:, rows, :]

        if k > 0:
            edges[k].wait_recv()
        edge_cols[...] = lax.dot_general(edge_in[s], eye, TN, preferred_element_type=jnp.float32)

        def body(i, carry, base=base):
            at = pl.ds(pl.multiple_of(base + i * 16, 16), 16)
            cols = edge_cols[pl.ds(pl.multiple_of(i * 16, 16), 16), :]

            def column(f, c):
                before = jnp.where(at_first, jnp.where(outer_first, f, cols[:, 2 * c:2 * c + 1]), pltpu.roll(f, 1, 1))
                after = jnp.where(at_last, jnp.where(outer_last, f, cols[:, 2 * c + 1:2 * c + 2]),
                                  pltpu.roll(f, wb - 1, 1))
                return (after - before) * col_scale

            def row(c):
                return (below[c, at, :].astype(jnp.float32) - above[c, at, :].astype(jnp.float32)) * row_scale

            s_ref[0, at, :] = column(center[0, at, :].astype(jnp.float32), 0).astype(jnp.bfloat16)
            s_ref[1, at, :] = row(1).astype(jnp.bfloat16)
            s_ref[2, at, :] = (0.5 * (row(0) + column(center[1, at, :].astype(jnp.float32), 1))).astype(jnp.bfloat16)
            return carry

        lax.fori_loop(0, fb // 16, body, 0)

    index = 0
    for i in range(frames // BLOCK):
        width = (i + 1) * BLOCK
        part = jnp.zeros((BLOCK, width), jnp.float32)
        for c in range(3):
            part += lax.dot_general(s_ref[c, i * BLOCK:(i + 1) * BLOCK, :], s_ref[c, :width, :], NT,
                                    preferred_element_type=jnp.float32)
        for j in range(i + 1):
            acc[index * BLOCK:(index + 1) * BLOCK, :] = part[:, j * BLOCK:(j + 1) * BLOCK]
            index += 1

    lo, place, waits, trail = 0, 0, [], []
    for n, (axis, distance, size, halved) in enumerate(stages):
        me = z if axis == "frame" else t
        bit = (me // distance) % 2
        peer = me + distance * (1 - 2 * bit)
        keep = lo + bit * size if halved else lo
        give = lo + (1 - bit) * size if halved else lo
        copy = pltpu.make_async_remote_copy(
            src_ref=acc.at[pl.ds(pl.multiple_of(give, 8), size), :], dst_ref=landing.at[place:place + size, :],
            send_sem=sum_send.at[n], recv_sem=sum_recv.at[n],
            device_id={axis: peer}, device_id_type=MESH)
        copy.start()
        copy.wait()
        at = pl.ds(pl.multiple_of(keep, 8), size)
        acc[at, :] = acc[at, :] + landing[place:place + size, :]
        if halved:
            trail.append((axis, peer, size, keep, lo))
        lo = keep
        place += size
    size = stages[-1][2]
    at = pl.ds(pl.multiple_of(lo, 8), size)
    total[at, :] = acc[at, :]
    for m, (axis, peer, size, keep, lo) in enumerate(reversed(trail)):
        n = len(stages) + m
        at = pl.ds(pl.multiple_of(keep, 8), size)
        copy = pltpu.make_async_remote_copy(
            src_ref=total.at[at, :], dst_ref=total.at[at, :],
            send_sem=sum_send.at[n], recv_sem=sum_recv.at[n],
            device_id={axis: peer}, device_id_type=MESH)
        copy.start()
        copy.wait()
    gram_ref[...] = total[...]

    for k in range(nz):
        up, dn, _ = halos[k]
        if k > 0:
            blocks[k].wait_send()
            edges[k].wait_send()

        @pl.when(t < nt - 1)
        def _(up=up):
            up.wait_send()

        @pl.when(t > 0)
        def _(dn=dn):
            dn.wait_send()


def exchange(x, nz, nt):
    fb, width = x.shape[1], x.shape[2]
    wb, frames = width // nz, fb * nz
    nb = frames // BLOCK
    rows = nb * (nb + 1) // 2 * BLOCK
    stages = sum_stages(nz, nt, rows)
    landing = sum(stage[2] for stage in stages)
    dma = pltpu.SemaphoreType.DMA
    vmem = pl.BlockSpec(memory_space=pltpu.VMEM)
    return pl.pallas_call(
        functools.partial(exchange_kernel, nz, nt, stages),
        out_shape=(jax.ShapeDtypeStruct((rows, BLOCK), jnp.float32),
                   jax.ShapeDtypeStruct((3, frames, wb), jnp.bfloat16)),
        in_specs=[vmem],
        out_specs=(vmem, vmem),
        scratch_shapes=[
            pltpu.VMEM((2, frames, wb), jnp.bfloat16),
            pltpu.VMEM((2, frames, wb), jnp.bfloat16),
            pltpu.VMEM((2, frames, wb), jnp.bfloat16),
            pltpu.VMEM((nz, 16, fb), jnp.bfloat16),
            pltpu.VMEM((nz, 16, fb), jnp.bfloat16),
            pltpu.VMEM((fb, 128), jnp.float32),
            pltpu.VMEM((rows, BLOCK), jnp.float32),
            pltpu.VMEM((landing, BLOCK), jnp.float32),
            pltpu.VMEM((rows, BLOCK), jnp.float32),
            dma, dma((nz,)), dma((nz,)), dma((nz,)), dma((nz,)),
            dma((nz,)), dma((nz,)), dma((nz,)), dma((nz,)),
            dma((2 * len(stages),)), dma((2 * len(stages),)),
        ],
        compiler_params=pltpu.CompilerParams(
            collective_id=0, has_side_effects=True, vmem_limit_bytes=40 * 1024 * 1024),
    )(x)


def factor_block(a):
    n = a.shape[0]
    row8 = lax.broadcasted_iota(jnp.int32, (8, n), 0)
    lane8 = lax.broadcasted_iota(jnp.int32, (8, n), 1)
    left = [a[8 * i:8 * i + 8, :] for i in range(n // 8)]
    right = [jnp.where(row8 + 8 * i == lane8, 1.0, 0.0) for i in range(n // 8)]
    for j in range(n):
        home, sub = j // 8, j % 8
        pivot = jnp.broadcast_to(left[home][sub:sub + 1, j:j + 1], (8, n))
        r = lax.rsqrt(pivot)
        u = jnp.broadcast_to(left[home][sub:sub + 1, :], (8, n)) * r
        m = jnp.broadcast_to(right[home][sub:sub + 1, :], (8, n)) * r
        for i in range(home, n // 8):
            c = jnp.broadcast_to(left[i][:, j:j + 1], (8, n)) * r
            new_left, new_right = left[i] - c * u, right[i] - c * m
            if i == home:
                new_left = jnp.where(row8 > sub, new_left, jnp.where(row8 == sub, u, left[i]))
                new_right = jnp.where(row8 > sub, new_right, jnp.where(row8 == sub, m, right[i]))
            left[i], right[i] = new_left, new_right
    return jnp.concatenate(left, axis=0), jnp.concatenate(right, axis=0)


def basis_kernel(scale, g_ref, s_ref, basis_ref, factor_ref, work, high, low):
    n = factor_ref.shape[0]
    nb = n // BLOCK
    row = lax.broadcasted_iota(jnp.int32, (BLOCK, BLOCK), 0)
    col = lax.broadcasted_iota(jnp.int32, (BLOCK, BLOCK), 1)

    work[...] = jnp.zeros_like(work)
    index = 0
    for i in range(nb):
        for j in range(i + 1):
            block = g_ref[index * BLOCK:(index + 1) * BLOCK, :]
            work[j, :, i * BLOCK:(i + 1) * BLOCK] = block.T
            index += 1
        work[i, :, n + i * BLOCK:n + (i + 1) * BLOCK] = jnp.where(row == col, 1.0, 0.0)

    def step(k, carry):
        diag = pl.ds(pl.multiple_of(k * BLOCK, BLOCK), BLOCK)
        upper, inverse = factor_block(work[k, :, diag])
        strip = jnp.dot(inverse, work[k], precision=EXACT, preferred_element_type=jnp.float32)
        work[k] = strip
        work[k, :, diag] = jnp.where(row <= col, upper, 0.0)
        for i in range(1, nb):
            @pl.when(i > k)
            def _(i=i):
                work[i] = work[i] - lax.dot_general(
                    work[k, :, i * BLOCK:(i + 1) * BLOCK], work[k], TN, precision=EXACT,
                    preferred_element_type=jnp.float32)
        return carry

    lax.fori_loop(0, nb, step, 0)

    for i in range(nb):
        for j in range(nb):
            at = slice(j * BLOCK, (j + 1) * BLOCK)
            block = work[i, :, at] * (1.0 / scale) if j >= i else jnp.zeros((BLOCK, BLOCK), jnp.float32)
            factor_ref[i * BLOCK:(i + 1) * BLOCK, at] = block
        m = work[i, :, n:2 * n] * scale
        head = m.astype(jnp.bfloat16)
        high[i] = head
        low[i] = (m - head.astype(jnp.float32)).astype(jnp.bfloat16)
    for c in range(3):
        for i in range(nb):
            depth = (i + 1) * BLOCK
            s = s_ref[c, :depth, :]
            value = jnp.dot(high[i, :, :depth], s, preferred_element_type=jnp.float32)
            value += jnp.dot(low[i, :, :depth], s, preferred_element_type=jnp.float32)
            basis_ref[c, i * BLOCK:(i + 1) * BLOCK, :] = value.astype(jnp.bfloat16)


def orthonormal(gram, strain, scale):
    frames = strain.shape[1]
    nb = frames // BLOCK
    vmem = pl.BlockSpec(memory_space=pltpu.VMEM)
    return pl.pallas_call(
        functools.partial(basis_kernel, scale),
        out_shape=(jax.ShapeDtypeStruct(strain.shape, jnp.bfloat16),
                   jax.ShapeDtypeStruct((frames, frames), jnp.float32)),
        in_specs=[vmem, vmem],
        out_specs=(vmem, vmem),
        scratch_shapes=[
            pltpu.VMEM((nb, BLOCK, 2 * frames), jnp.float32),
            pltpu.VMEM((nb, BLOCK, frames), jnp.bfloat16),
            pltpu.VMEM((nb, BLOCK, frames), jnp.bfloat16),
        ],
        compiler_params=pltpu.CompilerParams(vmem_limit_bytes=40 * 1024 * 1024),
    )(gram, strain)


def local(nz, nt, displacement):
    frames, rows, width = displacement.shape[0] * nz, displacement.shape[2] * nt, displacement.shape[3]
    scale = math.sqrt(3 * rows * width)
    x = jnp.transpose(displacement[:, :, 0, :], (1, 0, 2))
    gram, strain = exchange(x, nz, nt)
    basis, factor = orthonormal(gram, strain, scale)
    return jnp.transpose(basis, (1, 0, 2))[:, :, None, :], factor


def solution(mesh):
    return jax.shard_map(
        functools.partial(local, mesh.shape["frame"], mesh.shape["tile"]),
        mesh=mesh,
        in_specs=(P("frame", None, "tile", None),),
        out_specs=(P(None, None, "tile", "frame"), P()),
        check_vma=False,
    )
```

```python
import functools
import math

import jax
import jax.numpy as jnp
from jax import lax
from jax.experimental import pallas as pl
from jax.experimental.pallas import tpu as pltpu
from jax.sharding import PartitionSpec as P

MESH = pl.DeviceIdType.MESH
BLOCK = 128
PIECES = 4
GROUP = 8
NT = (((1,), (1,)), ((), ()))
TN = (((0,), (0,)), ((), ()))
EXACT = lax.Precision.HIGHEST


def sum_stages(nz, nt, rows):
    stages = []
    for name, peers in (("core", 2), ("chip", nt // 2), ("frame", nz)):
        split = rows % (8 * peers) == 0
        rows = rows // peers if split else rows
        stages.append((name, peers, rows, split))
    return stages


def exchange_kernel(nz, nt, stages, x_ref, gram_ref, s_ref, center, above, below, edge_out, edge_in,
                    edge_cols, acc, landing, total, own_sem, a2a_send, a2a_recv, edge_send, edge_recv,
                    up_send, up_recv, dn_send, dn_recv, sum_send, sum_recv):
    z, t = lax.axis_index("frame"), lax.axis_index("tile")
    fb, wb = x_ref.shape[1], x_ref.shape[2] // nz
    frames, part = fb * nz, fb // PIECES
    chips = nt // 2
    core, chip = t % 2, t // 2

    def member(name, k):
        if name == "core":
            return core, lax.rem(core + k, 2), {"tile": chip * 2 + lax.rem(core + k, 2)}
        if name == "chip":
            return chip, lax.rem(chip + k, chips), {"tile": lax.rem(chip + k, chips) * 2 + core}
        return z, lax.rem(z + k, nz), {"frame": lax.rem(z + k, nz)}

    barrier = pltpu.get_barrier_semaphore()
    greeted = 0
    for name, peers in (("core", 2), ("chip", chips), ("frame", nz)):
        for k in range(1, peers):
            pl.semaphore_signal(barrier, inc=1, device_id=member(name, k)[2], device_id_type=MESH)
            greeted += 1
    for k in (1, nt - 1):
        pl.semaphore_signal(barrier, inc=1, device_id={"tile": lax.rem(t + k, nt)}, device_id_type=MESH)
        greeted += 1
    pl.semaphore_wait(barrier, greeted)

    def frame_rows(s, p):
        return pl.ds(pl.multiple_of(s * fb + p * part, 16), part)

    own_cols = pl.ds(pl.multiple_of(z * wb, 128), wb)
    own = pltpu.make_async_copy(
        x_ref.at[:, :, own_cols], center.at[:, pl.ds(pl.multiple_of(z * fb, 16), fb), :], own_sem)
    own.start()
    blocks = {}

    def send_piece(p):
        for k in range(1, nz):
            d = lax.rem(z + k, nz)
            copy = pltpu.make_async_remote_copy(
                src_ref=x_ref.at[:, p * part:(p + 1) * part, pl.ds(pl.multiple_of(d * wb, 128), wb)],
                dst_ref=center.at[:, frame_rows(z, p), :],
                send_sem=a2a_send.at[k, p], recv_sem=a2a_recv.at[k, p],
                device_id={"frame": d}, device_id_type=MESH)
            copy.start()
            blocks[k, p] = copy

    halos = {}

    def send_halo(k, p):
        s = lax.rem(z - k + nz, nz)
        rows = frame_rows(s, p)
        src = x_ref.at[:, p * part:(p + 1) * part, own_cols] if k == 0 else center.at[:, rows, :]
        up = pltpu.make_async_remote_copy(
            src_ref=src, dst_ref=above.at[:, rows, :],
            send_sem=up_send.at[k, p], recv_sem=up_recv.at[k, p],
            device_id={"tile": lax.rem(t + 1, nt)}, device_id_type=MESH)
        dn = pltpu.make_async_remote_copy(
            src_ref=src, dst_ref=below.at[:, rows, :],
            send_sem=dn_send.at[k, p], recv_sem=dn_recv.at[k, p],
            device_id={"tile": lax.rem(t + nt - 1, nt)}, device_id_type=MESH)
        halos[k, p] = (up, dn, s)

        @pl.when(t < nt - 1)
        def _():
            up.start()

        @pl.when(t > 0)
        def _():
            dn.start()

    send_piece(0)
    for p in range(PIECES):
        send_halo(0, p)

    row16 = lax.broadcasted_iota(jnp.int32, (16, 128), 0)
    lane16 = lax.broadcasted_iota(jnp.int32, (16, 128), 1)

    def pick(row, lane):
        return jnp.where((row16 == row) & (lane16 == lane), 1.0, 0.0).astype(jnp.bfloat16)

    for d in range(nz):
        total_edge = jnp.zeros((16, fb), jnp.float32)
        for c in range(2):
            if d > 0:
                total_edge += lax.dot_general(pick(2 * c, 127), x_ref[c, :, d * wb - 128:d * wb], NT,
                                              preferred_element_type=jnp.float32)
            if d < nz - 1:
                total_edge += lax.dot_general(pick(2 * c + 1, 0), x_ref[c, :, (d + 1) * wb:(d + 1) * wb + 128], NT,
                                              preferred_element_type=jnp.float32)
        edge_out[d] = total_edge.astype(jnp.bfloat16)
    edges = [None]
    for k in range(1, nz):
        d = lax.rem(z + k, nz)
        copy = pltpu.make_async_remote_copy(
            src_ref=edge_out.at[d], dst_ref=edge_in.at[z],
            send_sem=edge_send.at[k], recv_sem=edge_recv.at[k],
            device_id={"frame": d}, device_id_type=MESH)
        copy.start()
        edges.append(copy)
    edge_in[z] = edge_out[z]
    for p in range(1, PIECES):
        send_piece(p)
    own.wait()

    lane = lax.broadcasted_iota(jnp.int32, (16, wb), 1)
    outer_first, outer_last = (z == 0), (z == nz - 1)
    at_first, at_last = lane == 0, lane == wb - 1
    col_scale = jnp.where((at_first & outer_first) | (at_last & outer_last), 1.0, 0.5)
    row_scale = jnp.where((t == 0) | (t == nt - 1), 1.0, 0.5)
    eye = jnp.where(row16 == lane16, 1.0, 0.0).astype(jnp.bfloat16)

    def strain_piece(k, p):
        up, dn, s = halos[k, p]
        rows = frame_rows(s, p)

        @pl.when(t > 0)
        def _():
            up.wait_recv()

        @pl.when(t < nt - 1)
        def _():
            dn.wait_recv()

        @pl.when(t == 0)
        def _():
            above[:, rows, :] = center[:, rows, :]

        @pl.when(t == nt - 1)
        def _():
            below[:, rows, :] = center[:, rows, :]

        if p == 0:
            if k > 0:
                edges[k].wait_recv()
            edge_cols[k] = lax.dot_general(edge_in[s], eye, TN, preferred_element_type=jnp.float32)

        def body(i, carry):
            at = pl.ds(pl.multiple_of(s * fb + p * part + i * 16, 16), 16)
            cols = edge_cols[k, pl.ds(pl.multiple_of(p * part + i * 16, 16), 16), :]

            def column(f, c):
                before = jnp.where(at_first, jnp.where(outer_first, f, cols[:, 2 * c:2 * c + 1]), pltpu.roll(f, 1, 1))
                after = jnp.where(at_last, jnp.where(outer_last, f, cols[:, 2 * c + 1:2 * c + 2]),
                                  pltpu.roll(f, wb - 1, 1))
                return (after - before) * col_scale

            def row(c):
                return (below[c, at, :].astype(jnp.float32) - above[c, at, :].astype(jnp.float32)) * row_scale

            s_ref[0, at, :] = column(center[0, at, :].astype(jnp.float32), 0).astype(jnp.bfloat16)
            s_ref[1, at, :] = row(1).astype(jnp.bfloat16)
            s_ref[2, at, :] = (0.5 * (row(0) + column(center[1, at, :].astype(jnp.float32), 1))).astype(jnp.bfloat16)
            return carry

        lax.fori_loop(0, part // 16, body, 0)

    for p in range(PIECES + 1):
        if p < PIECES:
            for k in range(1, nz):
                blocks[k, p].wait_recv()
                send_halo(k, p)
        if p > 0:
            for k in range(nz):
                strain_piece(k, p - 1)

    index = 0
    for i in range(frames // BLOCK):
        width = (i + 1) * BLOCK
        value = jnp.zeros((BLOCK, width), jnp.float32)
        for c in range(3):
            value += lax.dot_general(s_ref[c, i * BLOCK:(i + 1) * BLOCK, :], s_ref[c, :width, :], NT,
                                     preferred_element_type=jnp.float32)
        for j in range(i + 1):
            acc[index * BLOCK:(index + 1) * BLOCK, :] = value[:, j * BLOCK:(j + 1) * BLOCK]
            index += 1

    lo, place, slot, trail = 0, 0, 0, []
    for name, peers, size, split in stages:
        me = member(name, 0)[0]
        mine = pl.ds(pl.multiple_of(place + me * size, 8), size)
        copies = []
        for k in range(1, peers):
            _, index, device = member(name, k)
            give = lo + index * size if split else lo
            copy = pltpu.make_async_remote_copy(
                src_ref=acc.at[pl.ds(pl.multiple_of(give, 8), size), :], dst_ref=landing.at[mine, :],
                send_sem=sum_send.at[slot], recv_sem=sum_recv.at[slot],
                device_id=device, device_id_type=MESH)
            copy.start()
            copies.append(copy)
            slot += 1
        keep = lo + me * size if split else lo
        at = pl.ds(pl.multiple_of(keep, 8), size)
        landing[mine, :] = acc[at, :]
        for copy in copies:
            copy.wait()
        value = landing[place:place + size, :]
        for n in range(1, peers):
            value += landing[place + n * size:place + (n + 1) * size, :]
        acc[at, :] = value
        if split:
            trail.append((name, peers, size, keep))
        lo = keep
        place += peers * size
    at = pl.ds(pl.multiple_of(lo, 8), stages[-1][2])
    total[at, :] = acc[at, :]
    for name, peers, size, keep in reversed(trail):
        at = pl.ds(pl.multiple_of(keep, 8), size)
        copies = []
        for k in range(1, peers):
            copy = pltpu.make_async_remote_copy(
                src_ref=total.at[at, :], dst_ref=total.at[at, :],
                send_sem=sum_send.at[slot], recv_sem=sum_recv.at[slot],
                device_id=member(name, k)[2], device_id_type=MESH)
            copy.start()
            copies.append(copy)
            slot += 1
        for copy in copies:
            copy.wait()
    gram_ref[...] = total[...]

    for k in range(1, nz):
        edges[k].wait_send()
    for k in range(nz):
        for p in range(PIECES):
            up, dn, _ = halos[k, p]
            if k > 0:
                blocks[k, p].wait_send()

            @pl.when(t < nt - 1)
            def _(up=up):
                up.wait_send()

            @pl.when(t > 0)
            def _(dn=dn):
                dn.wait_send()


def exchange(x, nz, nt):
    fb, width = x.shape[1], x.shape[2]
    wb, frames = width // nz, fb * nz
    nb = frames // BLOCK
    rows = nb * (nb + 1) // 2 * BLOCK
    stages = sum_stages(nz, nt, rows)
    landing = sum(stage[1] * stage[2] for stage in stages)
    steps = 2 * sum(stage[1] - 1 for stage in stages)
    dma = pltpu.SemaphoreType.DMA
    vmem = pl.BlockSpec(memory_space=pltpu.VMEM)
    return pl.pallas_call(
        functools.partial(exchange_kernel, nz, nt, stages),
        out_shape=(jax.ShapeDtypeStruct((rows, BLOCK), jnp.float32),
                   jax.ShapeDtypeStruct((3, frames, wb), jnp.bfloat16)),
        in_specs=[vmem],
        out_specs=(vmem, vmem),
        scratch_shapes=[
            pltpu.VMEM((2, frames, wb), jnp.bfloat16),
            pltpu.VMEM((2, frames, wb), jnp.bfloat16),
            pltpu.VMEM((2, frames, wb), jnp.bfloat16),
            pltpu.VMEM((nz, 16, fb), jnp.bfloat16),
            pltpu.VMEM((nz, 16, fb), jnp.bfloat16),
            pltpu.VMEM((nz, fb, 128), jnp.float32),
            pltpu.VMEM((rows, BLOCK), jnp.float32),
            pltpu.VMEM((landing, BLOCK), jnp.float32),
            pltpu.VMEM((rows, BLOCK), jnp.float32),
            dma, dma((nz, PIECES)), dma((nz, PIECES)), dma((nz,)), dma((nz,)),
            dma((nz, PIECES)), dma((nz, PIECES)), dma((nz, PIECES)), dma((nz, PIECES)),
            dma((steps,)), dma((steps,)),
        ],
        compiler_params=pltpu.CompilerParams(
            collective_id=0, has_side_effects=True, vmem_limit_bytes=40 * 1024 * 1024),
    )(x)


def factor_block(a):
    n = a.shape[0]
    shape = (GROUP, n)
    row8 = lax.broadcasted_iota(jnp.int32, shape, 0)
    lane8 = lax.broadcasted_iota(jnp.int32, shape, 1)
    tiles = n // GROUP
    left = [a[GROUP * i:GROUP * (i + 1), :] for i in range(tiles)]
    right = [jnp.where(row8 + GROUP * i == lane8, 1.0, 0.0) for i in range(tiles)]

    def row_of(tile, p):
        return jnp.broadcast_to(tile[p:p + 1, :], shape)

    for g in range(tiles):
        first = GROUP * g
        columns = [jnp.broadcast_to(left[g][:, first + q:first + q + 1], shape) for q in range(GROUP)]
        entry = {(p, q): row_of(columns[q], p) for p in range(GROUP) for q in range(p + 1)}
        r = []
        for q in range(GROUP):
            r.append(lax.rsqrt(entry[q, q]))
            for p in range(q + 1, GROUP):
                entry[p, q] = entry[p, q] * r[q]
            for p in range(q + 1, GROUP):
                for m in range(q + 1, p + 1):
                    entry[p, m] = entry[p, m] - entry[p, q] * entry[m, q]
        tops = []
        for tile in (left[g], right[g]):
            rows = [row_of(tile, p) for p in range(GROUP)]
            for q in range(GROUP):
                rows[q] = rows[q] * r[q]
                for p in range(q + 1, GROUP):
                    rows[p] = rows[p] - entry[p, q] * rows[q]
            tops.append(rows)
        for i in range(g + 1, tiles):
            c = [jnp.broadcast_to(left[i][:, first + q:first + q + 1], shape) for q in range(GROUP)]
            for q in range(GROUP):
                c[q] = c[q] * r[q]
                for m in range(q + 1, GROUP):
                    c[m] = c[m] - c[q] * entry[m, q]
            for q in range(GROUP):
                left[i] = left[i] - c[q] * tops[0][q]
                right[i] = right[i] - c[q] * tops[1][q]
        packed = []
        for rows in tops:
            value = rows[0]
            for q in range(1, GROUP):
                value = jnp.where(row8 == q, rows[q], value)
            packed.append(value)
        left[g], right[g] = packed
    return jnp.concatenate(left, axis=0), jnp.concatenate(right, axis=0)


def basis_kernel(scale, g_ref, s_ref, basis_ref, factor_ref, work, planes):
    n = factor_ref.shape[0]
    wide = n // 2
    nb = n // BLOCK
    row = lax.broadcasted_iota(jnp.int32, (BLOCK, BLOCK), 0)
    col = lax.broadcasted_iota(jnp.int32, (BLOCK, BLOCK), 1)

    work[...] = jnp.zeros_like(work)
    index = 0
    for i in range(nb):
        for j in range(i + 1):
            block = g_ref[index * BLOCK:(index + 1) * BLOCK, :]
            work[j, :, i * BLOCK:(i + 1) * BLOCK] = block.T
            index += 1
        work[i, :, n + i * BLOCK:n + (i + 1) * BLOCK] = jnp.where(row == col, 1.0, 0.0)

    def step(k, carry):
        diag = pl.ds(pl.multiple_of(k * BLOCK, BLOCK), BLOCK)
        upper, inverse = factor_block(work[k, :, diag])
        window = pl.ds(pl.multiple_of(k * BLOCK, BLOCK), n + BLOCK)
        strip = jnp.dot(inverse, work[k, :, window], precision=EXACT, preferred_element_type=jnp.float32)
        work[k, :, window] = strip
        work[k, :, diag] = jnp.where(row <= col, upper, 0.0)
        for i in range(1, nb):
            @pl.when(i > k)
            def _(i=i):
                work[i, :, window] = work[i, :, window] - lax.dot_general(
                    work[k, :, i * BLOCK:(i + 1) * BLOCK], work[k, :, window], TN, precision=EXACT,
                    preferred_element_type=jnp.float32)
        return carry

    lax.fori_loop(0, nb, step, 0)

    for i in range(nb):
        for j in range(nb):
            at = slice(j * BLOCK, (j + 1) * BLOCK)
            block = work[i, :, at] * (1.0 / scale) if j >= i else jnp.zeros((BLOCK, BLOCK), jnp.float32)
            factor_ref[i * BLOCK:(i + 1) * BLOCK, at] = block
        m = work[i, :, n:2 * n] * scale
        head = m.astype(jnp.bfloat16)
        half, at = i * BLOCK // wide, (i * BLOCK) % wide
        planes[half, at:at + BLOCK, :] = head
        planes[half, wide + at:wide + at + BLOCK, :] = (m - head.astype(jnp.float32)).astype(jnp.bfloat16)
    for c in range(3):
        for i in range(n // wide):
            depth = (i + 1) * wide
            value = jnp.dot(planes[i, :, :depth], s_ref[c, :depth, :], preferred_element_type=jnp.float32)
            basis_ref[c, i * wide:(i + 1) * wide, :] = (value[:wide] + value[wide:]).astype(jnp.bfloat16)


def orthonormal(gram, strain, scale):
    frames = strain.shape[1]
    nb = frames // BLOCK
    vmem = pl.BlockSpec(memory_space=pltpu.VMEM)
    return pl.pallas_call(
        functools.partial(basis_kernel, scale),
        out_shape=(jax.ShapeDtypeStruct(strain.shape, jnp.bfloat16),
                   jax.ShapeDtypeStruct((frames, frames), jnp.float32)),
        in_specs=[vmem, vmem],
        out_specs=(vmem, vmem),
        scratch_shapes=[
            pltpu.VMEM((nb, BLOCK, 2 * frames), jnp.float32),
            pltpu.VMEM((2, frames, frames), jnp.bfloat16),
        ],
        compiler_params=pltpu.CompilerParams(vmem_limit_bytes=40 * 1024 * 1024),
    )(gram, strain)


def local(nz, nt, displacement):
    frames, rows, width = displacement.shape[0] * nz, displacement.shape[2] * nt, displacement.shape[3]
    scale = math.sqrt(3 * rows * width)
    x = jnp.transpose(displacement[:, :, 0, :], (1, 0, 2))
    gram, strain = exchange(x, nz, nt)
    basis, factor = orthonormal(gram, strain, scale)
    return jnp.transpose(basis, (1, 0, 2))[:, :, None, :], factor


def solution(mesh):
    return jax.shard_map(
        functools.partial(local, mesh.shape["frame"], mesh.shape["tile"]),
        mesh=mesh,
        in_specs=(P("frame", None, "tile", None),),
        out_specs=(P(None, None, "tile", "frame"), P()),
        check_vma=False,
    )
```

```python
import functools
import math

import jax
import jax.numpy as jnp
from jax import lax
from jax.experimental import pallas as pl
from jax.experimental.pallas import tpu as pltpu
from jax.sharding import PartitionSpec as P

MESH = pl.DeviceIdType.MESH
BLOCK = 128
PIECE = 16
AHEAD = 3
GROUP = 8
NT = (((1,), (1,)), ((), ()))
TN = (((0,), (0,)), ((), ()))
EXACT = lax.Precision.HIGHEST


def sum_stages(nz, nt, rows):
    stages = []
    for name, peers in (("core", 2), ("chip", nt // 2), ("frame", nz)):
        split = rows % (8 * peers) == 0
        rows = rows // peers if split else rows
        stages.append((name, peers, rows, split))
    return stages


def exchange_kernel(nz, nt, stages, x_ref, gram_ref, s_ref, center, above, below, edge_out, edge_in,
                    edge_cols, acc, landing, total, own_sem, a2a_send, a2a_recv, edge_send, edge_recv,
                    up_send, up_recv, dn_send, dn_recv, sum_send, sum_recv):
    z, t = lax.axis_index("frame"), lax.axis_index("tile")
    fb, wb = x_ref.shape[1], x_ref.shape[2] // nz
    frames, part, pieces = fb * nz, PIECE, fb // PIECE
    chips = nt // 2
    core, chip = t % 2, t // 2

    def member(name, k):
        if name == "core":
            return core, lax.rem(core + k, 2), {"tile": chip * 2 + lax.rem(core + k, 2)}
        if name == "chip":
            return chip, lax.rem(chip + k, chips), {"tile": lax.rem(chip + k, chips) * 2 + core}
        return z, lax.rem(z + k, nz), {"frame": lax.rem(z + k, nz)}

    barrier = pltpu.get_barrier_semaphore()
    greeted = 0
    for name, peers in (("core", 2), ("chip", chips), ("frame", nz)):
        for k in range(1, peers):
            pl.semaphore_signal(barrier, inc=1, device_id=member(name, k)[2], device_id_type=MESH)
            greeted += 1
    for k in (1, nt - 1):
        pl.semaphore_signal(barrier, inc=1, device_id={"tile": lax.rem(t + k, nt)}, device_id_type=MESH)
        greeted += 1
    pl.semaphore_wait(barrier, greeted)

    def frame_rows(s, p):
        return pl.ds(pl.multiple_of(s * fb + p * part, 16), part)

    own_cols = pl.ds(pl.multiple_of(z * wb, 128), wb)
    own = pltpu.make_async_copy(
        x_ref.at[:, :, own_cols], center.at[:, pl.ds(pl.multiple_of(z * fb, 16), fb), :], own_sem)
    own.start()
    blocks = {}

    def send_piece(p):
        for k in range(1, nz):
            d = lax.rem(z + k, nz)
            copy = pltpu.make_async_remote_copy(
                src_ref=x_ref.at[:, p * part:(p + 1) * part, pl.ds(pl.multiple_of(d * wb, 128), wb)],
                dst_ref=center.at[:, frame_rows(z, p), :],
                send_sem=a2a_send.at[k, p], recv_sem=a2a_recv.at[k, p],
                device_id={"frame": d}, device_id_type=MESH)
            copy.start()
            blocks[k, p] = copy

    halos = {}

    def send_halo(k, p):
        s = lax.rem(z - k + nz, nz)
        rows = frame_rows(s, p)
        src = x_ref.at[:, p * part:(p + 1) * part, own_cols] if k == 0 else center.at[:, rows, :]
        up = pltpu.make_async_remote_copy(
            src_ref=src, dst_ref=above.at[:, rows, :],
            send_sem=up_send.at[k, p], recv_sem=up_recv.at[k, p],
            device_id={"tile": lax.rem(t + 1, nt)}, device_id_type=MESH)
        dn = pltpu.make_async_remote_copy(
            src_ref=src, dst_ref=below.at[:, rows, :],
            send_sem=dn_send.at[k, p], recv_sem=dn_recv.at[k, p],
            device_id={"tile": lax.rem(t + nt - 1, nt)}, device_id_type=MESH)
        halos[k, p] = (up, dn, s)

        @pl.when(t < nt - 1)
        def _():
            up.start()

        @pl.when(t > 0)
        def _():
            dn.start()

    row16 = lax.broadcasted_iota(jnp.int32, (16, 128), 0)
    lane16 = lax.broadcasted_iota(jnp.int32, (16, 128), 1)

    def pick(row, lane):
        return jnp.where((row16 == row) & (lane16 == lane), 1.0, 0.0).astype(jnp.bfloat16)

    edges = [None]

    def send_edges():
        for d in range(nz):
            total_edge = jnp.zeros((16, fb), jnp.float32)
            for c in range(2):
                if d > 0:
                    total_edge += lax.dot_general(pick(2 * c, 127), x_ref[c, :, d * wb - 128:d * wb], NT,
                                                  preferred_element_type=jnp.float32)
                if d < nz - 1:
                    total_edge += lax.dot_general(pick(2 * c + 1, 0), x_ref[c, :, (d + 1) * wb:(d + 1) * wb + 128], NT,
                                                  preferred_element_type=jnp.float32)
            edge_out[d] = total_edge.astype(jnp.bfloat16)
        for k in range(1, nz):
            d = lax.rem(z + k, nz)
            copy = pltpu.make_async_remote_copy(
                src_ref=edge_out.at[d], dst_ref=edge_in.at[z],
                send_sem=edge_send.at[k], recv_sem=edge_recv.at[k],
                device_id={"frame": d}, device_id_type=MESH)
            copy.start()
            edges.append(copy)
        edge_in[z] = edge_out[z]

    for p in range(min(AHEAD, pieces)):
        send_piece(p)
        send_halo(0, p)
        if p == 0:
            send_edges()

    own.wait()

    lane = lax.broadcasted_iota(jnp.int32, (16, wb), 1)
    outer_first, outer_last = (z == 0), (z == nz - 1)
    at_first, at_last = lane == 0, lane == wb - 1
    col_scale = jnp.where((at_first & outer_first) | (at_last & outer_last), 1.0, 0.5)
    row_scale = jnp.where((t == 0) | (t == nt - 1), 1.0, 0.5)
    eye = jnp.where(row16 == lane16, 1.0, 0.0).astype(jnp.bfloat16)

    def strain_piece(p):
        for k in range(nz):
            up, dn, s = halos[k, p]

            @pl.when(t > 0)
            def _(up=up):
                up.wait_recv()

            @pl.when(t < nt - 1)
            def _(dn=dn):
                dn.wait_recv()

            if p == 0:
                if k > 0:
                    edges[k].wait_recv()
                edge_cols[k] = lax.dot_general(edge_in[s], eye, TN, preferred_element_type=jnp.float32)

        def body(k, carry):
            at = frame_rows(lax.rem(z - k + nz, nz), p)
            cols = edge_cols[k, p * part:(p + 1) * part, :]

            @pl.when(t == 0)
            def _():
                above[:, at, :] = center[:, at, :]

            @pl.when(t == nt - 1)
            def _():
                below[:, at, :] = center[:, at, :]

            def column(f, c):
                before = jnp.where(at_first, jnp.where(outer_first, f, cols[:, 2 * c:2 * c + 1]), pltpu.roll(f, 1, 1))
                after = jnp.where(at_last, jnp.where(outer_last, f, cols[:, 2 * c + 1:2 * c + 2]),
                                  pltpu.roll(f, wb - 1, 1))
                return (after - before) * col_scale

            def row(c):
                return (below[c, at, :].astype(jnp.float32) - above[c, at, :].astype(jnp.float32)) * row_scale

            s_ref[0, at, :] = column(center[0, at, :].astype(jnp.float32), 0).astype(jnp.bfloat16)
            s_ref[1, at, :] = row(1).astype(jnp.bfloat16)
            s_ref[2, at, :] = (0.5 * (row(0) + column(center[1, at, :].astype(jnp.float32), 1))).astype(jnp.bfloat16)
            return carry

        lax.fori_loop(0, nz, body, 0)

    for p in range(pieces + 1):
        if p < pieces:
            for k in range(1, nz):
                blocks[k, p].wait_recv()
                send_halo(k, p)
            if p + AHEAD < pieces:
                send_piece(p + AHEAD)
                send_halo(0, p + AHEAD)
        if p > 0:
            strain_piece(p - 1)

    packed = [(i, j) for i in range(frames // BLOCK) for j in range(i + 1)]
    half = len(packed) // 2

    def products(which):
        mine = packed[which * half:(which + 1) * half]
        for j0 in range(0, frames // BLOCK, 2):
            inside = [(i, j) for i, j in mine if j0 <= j < j0 + 2]
            if not inside:
                continue
            i0, i1 = min(inside)[0], max(inside)[0] + 1
            value = jnp.zeros(((i1 - i0) * BLOCK, 2 * BLOCK), jnp.float32)
            for c in range(3):
                value += lax.dot_general(s_ref[c, i0 * BLOCK:i1 * BLOCK, :],
                                         s_ref[c, j0 * BLOCK:(j0 + 2) * BLOCK, :], NT,
                                         preferred_element_type=jnp.float32)
            for i, j in inside:
                index = packed.index((i, j))
                acc[index * BLOCK:(index + 1) * BLOCK, :] = value[
                    (i - i0) * BLOCK:(i - i0 + 1) * BLOCK, (j - j0) * BLOCK:(j - j0 + 1) * BLOCK]

    def on_core(which, half_index):
        @pl.when(core == which)
        def _():
            products(half_index)

    on_core(0, 1)
    on_core(1, 0)

    lo, place, slot, trail = 0, 0, 0, []
    for name, peers, size, split in stages:
        me = member(name, 0)[0]
        mine = pl.ds(pl.multiple_of(place + me * size, 8), size)
        copies = []
        for k in range(1, peers):
            _, index, device = member(name, k)
            give = lo + index * size if split else lo
            copy = pltpu.make_async_remote_copy(
                src_ref=acc.at[pl.ds(pl.multiple_of(give, 8), size), :], dst_ref=landing.at[mine, :],
                send_sem=sum_send.at[slot], recv_sem=sum_recv.at[slot],
                device_id=device, device_id_type=MESH)
            copy.start()
            copies.append(copy)
            slot += 1
        if name == "core":
            on_core(0, 0)
            on_core(1, 1)
        keep = lo + me * size if split else lo
        at = pl.ds(pl.multiple_of(keep, 8), size)
        landing[mine, :] = acc[at, :]
        for copy in copies:
            copy.wait()
        value = landing[place:place + size, :]
        for n in range(1, peers):
            value += landing[place + n * size:place + (n + 1) * size, :]
        acc[at, :] = value
        if split:
            trail.append((name, peers, size, keep))
        lo = keep
        place += peers * size
    at = pl.ds(pl.multiple_of(lo, 8), stages[-1][2])
    total[at, :] = acc[at, :]
    for name, peers, size, keep in reversed(trail):
        at = pl.ds(pl.multiple_of(keep, 8), size)
        copies = []
        for k in range(1, peers):
            copy = pltpu.make_async_remote_copy(
                src_ref=total.at[at, :], dst_ref=total.at[at, :],
                send_sem=sum_send.at[slot], recv_sem=sum_recv.at[slot],
                device_id=member(name, k)[2], device_id_type=MESH)
            copy.start()
            copies.append(copy)
            slot += 1
        for copy in copies:
            copy.wait()
    gram_ref[...] = total[...]

    for k in range(1, nz):
        edges[k].wait_send()
    for k in range(nz):
        for p in range(pieces):
            up, dn, _ = halos[k, p]
            if k > 0:
                blocks[k, p].wait_send()

            @pl.when(t < nt - 1)
            def _(up=up):
                up.wait_send()

            @pl.when(t > 0)
            def _(dn=dn):
                dn.wait_send()


def exchange(x, nz, nt):
    fb, width = x.shape[1], x.shape[2]
    wb, frames = width // nz, fb * nz
    nb, pieces = frames // BLOCK, fb // PIECE
    rows = nb * (nb + 1) // 2 * BLOCK
    stages = sum_stages(nz, nt, rows)
    landing = sum(stage[1] * stage[2] for stage in stages)
    steps = 2 * sum(stage[1] - 1 for stage in stages)
    dma = pltpu.SemaphoreType.DMA
    vmem = pl.BlockSpec(memory_space=pltpu.VMEM)
    return pl.pallas_call(
        functools.partial(exchange_kernel, nz, nt, stages),
        out_shape=(jax.ShapeDtypeStruct((rows, BLOCK), jnp.float32),
                   jax.ShapeDtypeStruct((3, frames, wb), jnp.bfloat16)),
        in_specs=[vmem],
        out_specs=(vmem, vmem),
        scratch_shapes=[
            pltpu.VMEM((2, frames, wb), jnp.bfloat16),
            pltpu.VMEM((2, frames, wb), jnp.bfloat16),
            pltpu.VMEM((2, frames, wb), jnp.bfloat16),
            pltpu.VMEM((nz, 16, fb), jnp.bfloat16),
            pltpu.VMEM((nz, 16, fb), jnp.bfloat16),
            pltpu.VMEM((nz, fb, 128), jnp.float32),
            pltpu.VMEM((rows, BLOCK), jnp.float32),
            pltpu.VMEM((landing, BLOCK), jnp.float32),
            pltpu.VMEM((rows, BLOCK), jnp.float32),
            dma, dma((nz, pieces)), dma((nz, pieces)), dma((nz,)), dma((nz,)),
            dma((nz, pieces)), dma((nz, pieces)), dma((nz, pieces)), dma((nz, pieces)),
            dma((steps,)), dma((steps,)),
        ],
        compiler_params=pltpu.CompilerParams(
            collective_id=0, has_side_effects=True, vmem_limit_bytes=40 * 1024 * 1024),
    )(x)


def factor_block(a):
    n = a.shape[0]
    shape = (GROUP, n)
    row8 = lax.broadcasted_iota(jnp.int32, shape, 0)
    lane8 = lax.broadcasted_iota(jnp.int32, shape, 1)
    tiles = n // GROUP
    left = [a[GROUP * i:GROUP * (i + 1), :] for i in range(tiles)]
    right = [jnp.where(row8 + GROUP * i == lane8, 1.0, 0.0) for i in range(tiles)]

    def row_of(tile, p):
        return jnp.broadcast_to(tile[p:p + 1, :], shape)

    for g in range(tiles):
        first = GROUP * g
        columns = [jnp.broadcast_to(left[g][:, first + q:first + q + 1], shape) for q in range(GROUP)]
        entry = {(p, q): row_of(columns[q], p) for p in range(GROUP) for q in range(p + 1)}
        r = []
        for q in range(GROUP):
            r.append(lax.rsqrt(entry[q, q]))
            for p in range(q + 1, GROUP):
                entry[p, q] = entry[p, q] * r[q]
            for p in range(q + 1, GROUP):
                for m in range(q + 1, p + 1):
                    entry[p, m] = entry[p, m] - entry[p, q] * entry[m, q]
        tops = []
        for tile in (left[g], right[g]):
            rows = [row_of(tile, p) for p in range(GROUP)]
            for q in range(GROUP):
                rows[q] = rows[q] * r[q]
                for p in range(q + 1, GROUP):
                    rows[p] = rows[p] - entry[p, q] * rows[q]
            tops.append(rows)
        for i in range(g + 1, tiles):
            c = [jnp.broadcast_to(left[i][:, first + q:first + q + 1], shape) for q in range(GROUP)]
            for q in range(GROUP):
                c[q] = c[q] * r[q]
                for m in range(q + 1, GROUP):
                    c[m] = c[m] - c[q] * entry[m, q]
            for q in range(GROUP):
                left[i] = left[i] - c[q] * tops[0][q]
                right[i] = right[i] - c[q] * tops[1][q]
        packed = []
        for rows in tops:
            value = rows[0]
            for q in range(1, GROUP):
                value = jnp.where(row8 == q, rows[q], value)
            packed.append(value)
        left[g], right[g] = packed
    return jnp.concatenate(left, axis=0), jnp.concatenate(right, axis=0)


def basis_kernel(scale, g_ref, s_ref, basis_ref, factor_ref, work, planes):
    n = factor_ref.shape[0]
    wide = n // 2
    nb = n // BLOCK
    row = lax.broadcasted_iota(jnp.int32, (BLOCK, BLOCK), 0)
    col = lax.broadcasted_iota(jnp.int32, (BLOCK, BLOCK), 1)

    work[...] = jnp.zeros_like(work)
    index = 0
    for i in range(nb):
        for j in range(i + 1):
            block = g_ref[index * BLOCK:(index + 1) * BLOCK, :]
            work[j, :, i * BLOCK:(i + 1) * BLOCK] = block.T
            index += 1
        work[i, :, n + i * BLOCK:n + (i + 1) * BLOCK] = jnp.where(row == col, 1.0, 0.0)

    def step(k, carry):
        diag = pl.ds(pl.multiple_of(k * BLOCK, BLOCK), BLOCK)
        upper, inverse = factor_block(work[k, :, diag])
        window = pl.ds(pl.multiple_of(k * BLOCK, BLOCK), n + BLOCK)
        strip = jnp.dot(inverse, work[k, :, window], precision=EXACT, preferred_element_type=jnp.float32)
        work[k, :, window] = strip
        work[k, :, diag] = jnp.where(row <= col, upper, 0.0)
        for i in range(1, nb):
            @pl.when(i > k)
            def _(i=i):
                work[i, :, window] = work[i, :, window] - lax.dot_general(
                    work[k, :, i * BLOCK:(i + 1) * BLOCK], work[k, :, window], TN, precision=EXACT,
                    preferred_element_type=jnp.float32)
        return carry

    lax.fori_loop(0, nb, step, 0)

    for i in range(nb):
        for j in range(nb):
            at = slice(j * BLOCK, (j + 1) * BLOCK)
            block = work[i, :, at] * (1.0 / scale) if j >= i else jnp.zeros((BLOCK, BLOCK), jnp.float32)
            factor_ref[i * BLOCK:(i + 1) * BLOCK, at] = block
        m = work[i, :, n:2 * n] * scale
        head = m.astype(jnp.bfloat16)
        half, at = i * BLOCK // wide, (i * BLOCK) % wide
        planes[half, at:at + BLOCK, :] = head
        planes[half, wide + at:wide + at + BLOCK, :] = (m - head.astype(jnp.float32)).astype(jnp.bfloat16)
    for c in range(3):
        for i in range(n // wide):
            depth = (i + 1) * wide
            value = jnp.dot(planes[i, :, :depth], s_ref[c, :depth, :], preferred_element_type=jnp.float32)
            basis_ref[c, i * wide:(i + 1) * wide, :] = (value[:wide] + value[wide:]).astype(jnp.bfloat16)


def orthonormal(gram, strain, scale):
    frames = strain.shape[1]
    nb = frames // BLOCK
    vmem = pl.BlockSpec(memory_space=pltpu.VMEM)
    return pl.pallas_call(
        functools.partial(basis_kernel, scale),
        out_shape=(jax.ShapeDtypeStruct(strain.shape, jnp.bfloat16),
                   jax.ShapeDtypeStruct((frames, frames), jnp.float32)),
        in_specs=[vmem, vmem],
        out_specs=(vmem, vmem),
        scratch_shapes=[
            pltpu.VMEM((nb, BLOCK, 2 * frames), jnp.float32),
            pltpu.VMEM((2, frames, frames), jnp.bfloat16),
        ],
        compiler_params=pltpu.CompilerParams(vmem_limit_bytes=40 * 1024 * 1024),
    )(gram, strain)


def local(nz, nt, displacement):
    frames, rows, width = displacement.shape[0] * nz, displacement.shape[2] * nt, displacement.shape[3]
    scale = math.sqrt(3 * rows * width)
    x = jnp.transpose(displacement[:, :, 0, :], (1, 0, 2))
    gram, strain = exchange(x, nz, nt)
    basis, factor = orthonormal(gram, strain, scale)
    return jnp.transpose(basis, (1, 0, 2))[:, :, None, :], factor


def solution(mesh):
    return jax.shard_map(
        functools.partial(local, mesh.shape["frame"], mesh.shape["tile"]),
        mesh=mesh,
        in_specs=(P("frame", None, "tile", None),),
        out_specs=(P(None, None, "tile", "frame"), P()),
        check_vma=False,
    )
```

```python
import functools
import math

import jax
import jax.numpy as jnp
from jax import lax
from jax.experimental import pallas as pl
from jax.experimental.pallas import tpu as pltpu
from jax.sharding import PartitionSpec as P

MESH = pl.DeviceIdType.MESH
BLOCK = 128
PIECE = 16
AHEAD = 3
GROUP = 8
NT = (((1,), (1,)), ((), ()))
TN = (((0,), (0,)), ((), ()))
EXACT = lax.Precision.HIGHEST


def sum_stages(nz, nt, rows):
    stages = []
    for name, peers in (("core", 2), ("chip", nt // 2), ("frame", nz)):
        split = rows % (8 * peers) == 0
        rows = rows // peers if split else rows
        stages.append((name, peers, rows, split))
    return stages


def exchange_kernel(nz, nt, stages, x_ref, gram_ref, s_ref, center, above, below, edge_out, edge_in,
                    edge_cols, acc, landing, total, own_sem, a2a_send, a2a_recv, edge_send, edge_recv,
                    up_send, up_recv, dn_send, dn_recv, sum_send, sum_recv,
                    relay, x_send, x_recv, v_send, v_recv, f_send, f_recv):
    z, t = lax.axis_index("frame"), lax.axis_index("tile")
    fb, wb = x_ref.shape[1], x_ref.shape[2] // nz
    frames, part, pieces = fb * nz, PIECE, fb // PIECE
    chips = nt // 2
    core, chip = t % 2, t // 2

    def member(name, k):
        if name == "core":
            return core, lax.rem(core + k, 2), {"tile": chip * 2 + lax.rem(core + k, 2)}
        if name == "chip":
            return chip, lax.rem(chip + k, chips), {"tile": lax.rem(chip + k, chips) * 2 + core}
        return z, lax.rem(z + k, nz), {"frame": lax.rem(z + k, nz)}

    barrier = pltpu.get_barrier_semaphore()
    greeted = 0
    for name, me, peers in (("tile", t, nt), ("frame", z, nz)):
        for k in range(1, peers):
            pl.semaphore_signal(barrier, inc=1, device_id={name: lax.rem(me + k, peers)}, device_id_type=MESH)
            greeted += 1
    pl.semaphore_wait(barrier, greeted)

    def frame_rows(s, p):
        return pl.ds(pl.multiple_of(s * fb + p * part, 16), part)

    own_cols = pl.ds(pl.multiple_of(z * wb, 128), wb)
    own = pltpu.make_async_copy(
        x_ref.at[:, :, own_cols], center.at[:, pl.ds(pl.multiple_of(z * fb, 16), fb), :], own_sem)
    own.start()
    blocks = {}

    def send_piece(p):
        for k in range(1, nz):
            d = lax.rem(z + k, nz)
            copy = pltpu.make_async_remote_copy(
                src_ref=x_ref.at[:, p * part:(p + 1) * part, pl.ds(pl.multiple_of(d * wb, 128), wb)],
                dst_ref=center.at[:, frame_rows(z, p), :],
                send_sem=a2a_send.at[k, p], recv_sem=a2a_recv.at[k, p],
                device_id={"frame": d}, device_id_type=MESH)
            copy.start()
            blocks[k, p] = copy

    halos, corners = {}, {}
    corner = nt == 8
    low, high = nt // 2 - 1, nt // 2
    sends_up, sends_dn = t < nt - 1, t > 0
    gets_above, gets_below = t > 0, t < nt - 1
    if corner:
        sends_up, sends_dn = sends_up & (t != low), sends_dn & (t != high)
        gets_above, gets_below = gets_above & (t != high), gets_below & (t != low)

    def send_halo(k, p):
        s = lax.rem(z - k + nz, nz)
        rows = frame_rows(s, p)
        src = x_ref.at[:, p * part:(p + 1) * part, own_cols] if k == 0 else center.at[:, rows, :]
        up = pltpu.make_async_remote_copy(
            src_ref=src, dst_ref=above.at[:, rows, :],
            send_sem=up_send.at[k, p], recv_sem=up_recv.at[k, p],
            device_id={"tile": lax.rem(t + 1, nt)}, device_id_type=MESH)
        dn = pltpu.make_async_remote_copy(
            src_ref=src, dst_ref=below.at[:, rows, :],
            send_sem=dn_send.at[k, p], recv_sem=dn_recv.at[k, p],
            device_id={"tile": lax.rem(t + nt - 1, nt)}, device_id_type=MESH)
        halos[k, p] = (up, dn, s)

        @pl.when(sends_up)
        def _():
            up.start()

        @pl.when(sends_dn)
        def _():
            dn.start()

        if not corner:
            return

        def cross(target):
            return pltpu.make_async_remote_copy(
                src_ref=src.at[0], dst_ref=target.at[0, rows, :],
                send_sem=x_send.at[k, p], recv_sem=x_recv.at[k, p],
                device_id={"tile": nt - 1 - t}, device_id_type=MESH)

        def onward(target):
            return pltpu.make_async_remote_copy(
                src_ref=relay.at[rows, :], dst_ref=target.at[1, rows, :],
                send_sem=f_send.at[k, p], recv_sem=f_recv.at[k, p],
                device_id={"tile": low + t // (nt - 1)}, device_id_type=MESH)

        via = pltpu.make_async_remote_copy(
            src_ref=src.at[1], dst_ref=relay.at[rows, :],
            send_sem=v_send.at[k, p], recv_sem=v_recv.at[k, p],
            device_id={"tile": (nt - 1) * (high - t)}, device_id_type=MESH)
        corners[k, p] = (cross(above), cross(below), via, onward(above), onward(below))

        @pl.when(t == low)
        def _():
            via.start()
            corners[k, p][0].start()

        @pl.when(t == high)
        def _():
            via.start()
            corners[k, p][1].start()

    def forward(k, p):
        _, _, via, on_above, on_below = corners[k, p]

        @pl.when(t == nt - 1)
        def _():
            via.wait_recv()
            on_above.start()

        @pl.when(t == 0)
        def _():
            via.wait_recv()
            on_below.start()

    row16 = lax.broadcasted_iota(jnp.int32, (16, 128), 0)
    lane16 = lax.broadcasted_iota(jnp.int32, (16, 128), 1)

    def pick(row, lane):
        return jnp.where((row16 == row) & (lane16 == lane), 1.0, 0.0).astype(jnp.bfloat16)

    edges = [None]

    def send_edges():
        for d in range(nz):
            total_edge = jnp.zeros((16, fb), jnp.float32)
            for c in range(2):
                if d > 0:
                    total_edge += lax.dot_general(pick(2 * c, 127), x_ref[c, :, d * wb - 128:d * wb], NT,
                                                  preferred_element_type=jnp.float32)
                if d < nz - 1:
                    total_edge += lax.dot_general(pick(2 * c + 1, 0), x_ref[c, :, (d + 1) * wb:(d + 1) * wb + 128], NT,
                                                  preferred_element_type=jnp.float32)
            edge_out[d] = total_edge.astype(jnp.bfloat16)
        for k in range(1, nz):
            d = lax.rem(z + k, nz)
            copy = pltpu.make_async_remote_copy(
                src_ref=edge_out.at[d], dst_ref=edge_in.at[z],
                send_sem=edge_send.at[k], recv_sem=edge_recv.at[k],
                device_id={"frame": d}, device_id_type=MESH)
            copy.start()
            edges.append(copy)
        edge_in[z] = edge_out[z]

    for p in range(min(AHEAD, pieces)):
        send_piece(p)
        if p == 0:
            send_edges()
    for p in range(pieces):
        send_halo(0, p)

    own.wait()

    lane = lax.broadcasted_iota(jnp.int32, (16, wb), 1)
    outer_first, outer_last = (z == 0), (z == nz - 1)
    at_first, at_last = lane == 0, lane == wb - 1
    col_scale = jnp.where((at_first & outer_first) | (at_last & outer_last), 1.0, 0.5)
    row_scale = jnp.where((t == 0) | (t == nt - 1), 1.0, 0.5)
    eye = jnp.where(row16 == lane16, 1.0, 0.0).astype(jnp.bfloat16)

    def strain_piece(p):
        for k in range(nz):
            up, dn, s = halos[k, p]

            @pl.when(gets_above)
            def _(up=up):
                up.wait_recv()

            @pl.when(gets_below)
            def _(dn=dn):
                dn.wait_recv()

            if corner:
                over, under, _, on_above, on_below = corners[k, p]

                @pl.when(t == high)
                def _(over=over, on_above=on_above):
                    over.wait_recv()
                    on_above.wait_recv()

                @pl.when(t == low)
                def _(under=under, on_below=on_below):
                    under.wait_recv()
                    on_below.wait_recv()

            if p == 0:
                if k > 0:
                    edges[k].wait_recv()
                edge_cols[k] = lax.dot_general(edge_in[s], eye, TN, preferred_element_type=jnp.float32)

        def body(k, carry):
            at = frame_rows(lax.rem(z - k + nz, nz), p)
            cols = edge_cols[k, p * part:(p + 1) * part, :]

            @pl.when(t == 0)
            def _():
                above[:, at, :] = center[:, at, :]

            @pl.when(t == nt - 1)
            def _():
                below[:, at, :] = center[:, at, :]

            def column(f, c):
                before = jnp.where(at_first, jnp.where(outer_first, f, cols[:, 2 * c:2 * c + 1]), pltpu.roll(f, 1, 1))
                after = jnp.where(at_last, jnp.where(outer_last, f, cols[:, 2 * c + 1:2 * c + 2]),
                                  pltpu.roll(f, wb - 1, 1))
                return (after - before) * col_scale

            def row(c):
                return (below[c, at, :].astype(jnp.float32) - above[c, at, :].astype(jnp.float32)) * row_scale

            s_ref[0, at, :] = column(center[0, at, :].astype(jnp.float32), 0).astype(jnp.bfloat16)
            s_ref[1, at, :] = row(1).astype(jnp.bfloat16)
            s_ref[2, at, :] = (0.5 * (row(0) + column(center[1, at, :].astype(jnp.float32), 1))).astype(jnp.bfloat16)
            return carry

        lax.fori_loop(0, nz, body, 0)

    for p in range(pieces + 1):
        if p < pieces:
            for k in range(1, nz):
                blocks[k, p].wait_recv()
                send_halo(k, p)
            if p + AHEAD < pieces:
                send_piece(p + AHEAD)
        if p > 0:
            if corner:
                for k in range(nz):
                    forward(k, p - 1)
            strain_piece(p - 1)

    packed = [(i, j) for i in range(frames // BLOCK) for j in range(i + 1)]
    half = len(packed) // 2

    def products(which):
        mine = packed[which * half:(which + 1) * half]
        for j0 in range(0, frames // BLOCK, 2):
            inside = [(i, j) for i, j in mine if j0 <= j < j0 + 2]
            if not inside:
                continue
            i0, i1 = min(inside)[0], max(inside)[0] + 1
            value = jnp.zeros(((i1 - i0) * BLOCK, 2 * BLOCK), jnp.float32)
            for c in range(3):
                value += lax.dot_general(s_ref[c, i0 * BLOCK:i1 * BLOCK, :],
                                         s_ref[c, j0 * BLOCK:(j0 + 2) * BLOCK, :], NT,
                                         preferred_element_type=jnp.float32)
            for i, j in inside:
                index = packed.index((i, j))
                acc[index * BLOCK:(index + 1) * BLOCK, :] = value[
                    (i - i0) * BLOCK:(i - i0 + 1) * BLOCK, (j - j0) * BLOCK:(j - j0 + 1) * BLOCK]

    def on_core(which, half_index):
        @pl.when(core == which)
        def _():
            products(half_index)

    on_core(0, 1)
    on_core(1, 0)

    lo, place, slot, trail = 0, 0, 0, []
    for name, peers, size, split in stages:
        me = member(name, 0)[0]
        mine = pl.ds(pl.multiple_of(place + me * size, 8), size)
        copies = []
        for k in range(1, peers):
            _, index, device = member(name, k)
            give = lo + index * size if split else lo
            copy = pltpu.make_async_remote_copy(
                src_ref=acc.at[pl.ds(pl.multiple_of(give, 8), size), :], dst_ref=landing.at[mine, :],
                send_sem=sum_send.at[slot], recv_sem=sum_recv.at[slot],
                device_id=device, device_id_type=MESH)
            copy.start()
            copies.append(copy)
            slot += 1
        if name == "core":
            on_core(0, 0)
            on_core(1, 1)
        keep = lo + me * size if split else lo
        at = pl.ds(pl.multiple_of(keep, 8), size)
        landing[mine, :] = acc[at, :]
        for copy in copies:
            copy.wait()
        value = landing[place:place + size, :]
        for n in range(1, peers):
            value += landing[place + n * size:place + (n + 1) * size, :]
        acc[at, :] = value
        if split:
            trail.append((name, peers, size, keep))
        lo = keep
        place += peers * size
    at = pl.ds(pl.multiple_of(lo, 8), stages[-1][2])
    total[at, :] = acc[at, :]
    for name, peers, size, keep in reversed(trail):
        at = pl.ds(pl.multiple_of(keep, 8), size)
        copies = []
        for k in range(1, peers):
            copy = pltpu.make_async_remote_copy(
                src_ref=total.at[at, :], dst_ref=total.at[at, :],
                send_sem=sum_send.at[slot], recv_sem=sum_recv.at[slot],
                device_id=member(name, k)[2], device_id_type=MESH)
            copy.start()
            copies.append(copy)
            slot += 1
        for copy in copies:
            copy.wait()
    gram_ref[...] = total[...]

    for k in range(1, nz):
        edges[k].wait_send()
    for k in range(nz):
        for p in range(pieces):
            up, dn, _ = halos[k, p]
            if k > 0:
                blocks[k, p].wait_send()

            @pl.when(sends_up)
            def _(up=up):
                up.wait_send()

            @pl.when(sends_dn)
            def _(dn=dn):
                dn.wait_send()

            if corner:
                over, under, via, on_above, on_below = corners[k, p]

                @pl.when(t == low)
                def _(over=over, via=via):
                    over.wait_send()
                    via.wait_send()

                @pl.when(t == high)
                def _(under=under, via=via):
                    under.wait_send()
                    via.wait_send()

                @pl.when(t == nt - 1)
                def _(on_above=on_above):
                    on_above.wait_send()

                @pl.when(t == 0)
                def _(on_below=on_below):
                    on_below.wait_send()


def exchange(x, nz, nt):
    fb, width = x.shape[1], x.shape[2]
    wb, frames = width // nz, fb * nz
    nb, pieces = frames // BLOCK, fb // PIECE
    rows = nb * (nb + 1) // 2 * BLOCK
    stages = sum_stages(nz, nt, rows)
    landing = sum(stage[1] * stage[2] for stage in stages)
    steps = 2 * sum(stage[1] - 1 for stage in stages)
    dma = pltpu.SemaphoreType.DMA
    vmem = pl.BlockSpec(memory_space=pltpu.VMEM)
    return pl.pallas_call(
        functools.partial(exchange_kernel, nz, nt, stages),
        out_shape=(jax.ShapeDtypeStruct((rows, BLOCK), jnp.float32),
                   jax.ShapeDtypeStruct((3, frames, wb), jnp.bfloat16)),
        in_specs=[vmem],
        out_specs=(vmem, vmem),
        scratch_shapes=[
            pltpu.VMEM((2, frames, wb), jnp.bfloat16),
            pltpu.VMEM((2, frames, wb), jnp.bfloat16),
            pltpu.VMEM((2, frames, wb), jnp.bfloat16),
            pltpu.VMEM((nz, 16, fb), jnp.bfloat16),
            pltpu.VMEM((nz, 16, fb), jnp.bfloat16),
            pltpu.VMEM((nz, fb, 128), jnp.float32),
            pltpu.VMEM((rows, BLOCK), jnp.float32),
            pltpu.VMEM((landing, BLOCK), jnp.float32),
            pltpu.VMEM((rows, BLOCK), jnp.float32),
            dma, dma((nz, pieces)), dma((nz, pieces)), dma((nz,)), dma((nz,)),
            dma((nz, pieces)), dma((nz, pieces)), dma((nz, pieces)), dma((nz, pieces)),
            dma((steps,)), dma((steps,)),
            pltpu.VMEM((frames, wb), jnp.bfloat16),
            dma((nz, pieces)), dma((nz, pieces)), dma((nz, pieces)),
            dma((nz, pieces)), dma((nz, pieces)), dma((nz, pieces)),
        ],
        compiler_params=pltpu.CompilerParams(
            collective_id=0, has_side_effects=True, vmem_limit_bytes=40 * 1024 * 1024),
    )(x)


def factor_block(a):
    n = a.shape[0]
    shape = (GROUP, n)
    row8 = lax.broadcasted_iota(jnp.int32, shape, 0)
    lane8 = lax.broadcasted_iota(jnp.int32, shape, 1)
    tiles = n // GROUP
    left = [a[GROUP * i:GROUP * (i + 1), :] for i in range(tiles)]
    right = [jnp.where(row8 + GROUP * i == lane8, 1.0, 0.0) for i in range(tiles)]

    def row_of(tile, p):
        return jnp.broadcast_to(tile[p:p + 1, :], shape)

    for g in range(tiles):
        first = GROUP * g
        columns = [jnp.broadcast_to(left[g][:, first + q:first + q + 1], shape) for q in range(GROUP)]
        entry = {(p, q): row_of(columns[q], p) for p in range(GROUP) for q in range(p + 1)}
        r = []
        for q in range(GROUP):
            r.append(lax.rsqrt(entry[q, q]))
            for p in range(q + 1, GROUP):
                entry[p, q] = entry[p, q] * r[q]
            for p in range(q + 1, GROUP):
                for m in range(q + 1, p + 1):
                    entry[p, m] = entry[p, m] - entry[p, q] * entry[m, q]
        tops = []
        for tile in (left[g], right[g]):
            rows = [row_of(tile, p) for p in range(GROUP)]
            for q in range(GROUP):
                rows[q] = rows[q] * r[q]
                for p in range(q + 1, GROUP):
                    rows[p] = rows[p] - entry[p, q] * rows[q]
            tops.append(rows)
        for i in range(g + 1, tiles):
            c = [jnp.broadcast_to(left[i][:, first + q:first + q + 1], shape) for q in range(GROUP)]
            for q in range(GROUP):
                c[q] = c[q] * r[q]
                for m in range(q + 1, GROUP):
                    c[m] = c[m] - c[q] * entry[m, q]
            for q in range(GROUP):
                left[i] = left[i] - c[q] * tops[0][q]
                right[i] = right[i] - c[q] * tops[1][q]
        packed = []
        for rows in tops:
            value = rows[0]
            for q in range(1, GROUP):
                value = jnp.where(row8 == q, rows[q], value)
            packed.append(value)
        left[g], right[g] = packed
    return jnp.concatenate(left, axis=0), jnp.concatenate(right, axis=0)


def basis_kernel(scale, g_ref, s_ref, basis_ref, factor_ref, work, planes):
    n = factor_ref.shape[0]
    wide = n // 2
    nb = n // BLOCK
    row = lax.broadcasted_iota(jnp.int32, (BLOCK, BLOCK), 0)
    col = lax.broadcasted_iota(jnp.int32, (BLOCK, BLOCK), 1)

    work[...] = jnp.zeros_like(work)
    index = 0
    for i in range(nb):
        for j in range(i + 1):
            block = g_ref[index * BLOCK:(index + 1) * BLOCK, :]
            work[j, :, i * BLOCK:(i + 1) * BLOCK] = block.T
            index += 1
        work[i, :, n + i * BLOCK:n + (i + 1) * BLOCK] = jnp.where(row == col, 1.0, 0.0)

    def step(k, carry):
        diag = pl.ds(pl.multiple_of(k * BLOCK, BLOCK), BLOCK)
        upper, inverse = factor_block(work[k, :, diag])
        window = pl.ds(pl.multiple_of(k * BLOCK, BLOCK), n + BLOCK)
        strip = jnp.dot(inverse, work[k, :, window], precision=EXACT, preferred_element_type=jnp.float32)
        work[k, :, window] = strip
        work[k, :, diag] = jnp.where(row <= col, upper, 0.0)
        for i in range(1, nb):
            @pl.when(i > k)
            def _(i=i):
                work[i, :, window] = work[i, :, window] - lax.dot_general(
                    work[k, :, i * BLOCK:(i + 1) * BLOCK], work[k, :, window], TN, precision=EXACT,
                    preferred_element_type=jnp.float32)
        return carry

    lax.fori_loop(0, nb, step, 0)

    for i in range(nb):
        for j in range(nb):
            at = slice(j * BLOCK, (j + 1) * BLOCK)
            block = work[i, :, at] * (1.0 / scale) if j >= i else jnp.zeros((BLOCK, BLOCK), jnp.float32)
            factor_ref[i * BLOCK:(i + 1) * BLOCK, at] = block
        m = work[i, :, n:2 * n] * scale
        head = m.astype(jnp.bfloat16)
        half, at = i * BLOCK // wide, (i * BLOCK) % wide
        planes[half, at:at + BLOCK, :] = head
        planes[half, wide + at:wide + at + BLOCK, :] = (m - head.astype(jnp.float32)).astype(jnp.bfloat16)
    for c in range(3):
        for i in range(n // wide):
            depth = (i + 1) * wide
            value = jnp.dot(planes[i, :, :depth], s_ref[c, :depth, :], preferred_element_type=jnp.float32)
            basis_ref[c, i * wide:(i + 1) * wide, :] = (value[:wide] + value[wide:]).astype(jnp.bfloat16)


def orthonormal(gram, strain, scale):
    frames = strain.shape[1]
    nb = frames // BLOCK
    vmem = pl.BlockSpec(memory_space=pltpu.VMEM)
    return pl.pallas_call(
        functools.partial(basis_kernel, scale),
        out_shape=(jax.ShapeDtypeStruct(strain.shape, jnp.bfloat16),
                   jax.ShapeDtypeStruct((frames, frames), jnp.float32)),
        in_specs=[vmem, vmem],
        out_specs=(vmem, vmem),
        scratch_shapes=[
            pltpu.VMEM((nb, BLOCK, 2 * frames), jnp.float32),
            pltpu.VMEM((2, frames, frames), jnp.bfloat16),
        ],
        compiler_params=pltpu.CompilerParams(vmem_limit_bytes=40 * 1024 * 1024),
    )(gram, strain)


def local(nz, nt, displacement):
    frames, rows, width = displacement.shape[0] * nz, displacement.shape[2] * nt, displacement.shape[3]
    scale = math.sqrt(3 * rows * width)
    x = jnp.transpose(displacement[:, :, 0, :], (1, 0, 2))
    gram, strain = exchange(x, nz, nt)
    basis, factor = orthonormal(gram, strain, scale)
    return jnp.transpose(basis, (1, 0, 2))[:, :, None, :], factor


def solution(mesh):
    return jax.shard_map(
        functools.partial(local, mesh.shape["frame"], mesh.shape["tile"]),
        mesh=mesh,
        in_specs=(P("frame", None, "tile", None),),
        out_specs=(P(None, None, "tile", "frame"), P()),
        check_vma=False,
    )
```

```python
import functools
import math

import jax
import jax.numpy as jnp
from jax import lax
from jax.experimental import pallas as pl
from jax.experimental.pallas import tpu as pltpu
from jax.sharding import PartitionSpec as P

MESH = pl.DeviceIdType.MESH
BLOCK = 128
PIECE = 16
AHEAD = 3
GROUP = 8
NT = (((1,), (1,)), ((), ()))
TN = (((0,), (0,)), ((), ()))
EXACT = lax.Precision.HIGHEST


def sum_stages(nz, nt, rows):
    stages = []
    for name, peers in (("core", 2), ("chip", nt // 2), ("frame", nz)):
        split = rows % (8 * peers) == 0
        rows = rows // peers if split else rows
        stages.append((name, peers, rows, split))
    return stages


def exchange_kernel(nz, nt, stages, raw_ref, gram_ref, s_ref, x_ref, center, above, below, edge_out, edge_in,
                    edge_cols, acc, landing, total, own_sem, a2a_send, a2a_recv, edge_send, edge_recv,
                    up_send, up_recv, dn_send, dn_recv, sum_send, sum_recv):
    z, t = lax.axis_index("frame"), lax.axis_index("tile")
    fb, wb = x_ref.shape[1], x_ref.shape[2] // nz
    frames, part, pieces = fb * nz, PIECE, fb // PIECE
    chips = nt // 2
    core, chip = t % 2, t // 2

    def member(name, k):
        if name == "core":
            return core, lax.rem(core + k, 2), {"tile": chip * 2 + lax.rem(core + k, 2)}
        if name == "chip":
            return chip, lax.rem(chip + k, chips), {"tile": lax.rem(chip + k, chips) * 2 + core}
        return z, lax.rem(z + k, nz), {"frame": lax.rem(z + k, nz)}

    def separate(p):
        for c in range(2):
            x_ref[c, p * part:(p + 1) * part, :] = raw_ref[p * part:(p + 1) * part, c, :]

    barrier = pltpu.get_barrier_semaphore()
    greeted = 0
    for name, peers in (("core", 2), ("chip", chips), ("frame", nz)):
        for k in range(1, peers):
            pl.semaphore_signal(barrier, inc=1, device_id=member(name, k)[2], device_id_type=MESH)
            greeted += 1
    for k in (1, nt - 1):
        pl.semaphore_signal(barrier, inc=1, device_id={"tile": lax.rem(t + k, nt)}, device_id_type=MESH)
        greeted += 1
    for p in range(min(AHEAD, pieces)):
        separate(p)
    pl.semaphore_wait(barrier, greeted)

    def frame_rows(s, p):
        return pl.ds(pl.multiple_of(s * fb + p * part, 16), part)

    own_cols = pl.ds(pl.multiple_of(z * wb, 128), wb)
    blocks = {}

    def send_piece(p):
        for k in range(1, nz):
            d = lax.rem(z + k, nz)
            copy = pltpu.make_async_remote_copy(
                src_ref=x_ref.at[:, p * part:(p + 1) * part, pl.ds(pl.multiple_of(d * wb, 128), wb)],
                dst_ref=center.at[:, frame_rows(z, p), :],
                send_sem=a2a_send.at[k, p], recv_sem=a2a_recv.at[k, p],
                device_id={"frame": d}, device_id_type=MESH)
            copy.start()
            blocks[k, p] = copy

    halos = {}

    def send_halo(k, p):
        s = lax.rem(z - k + nz, nz)
        rows = frame_rows(s, p)
        src = x_ref.at[:, p * part:(p + 1) * part, own_cols] if k == 0 else center.at[:, rows, :]
        up = pltpu.make_async_remote_copy(
            src_ref=src, dst_ref=above.at[:, rows, :],
            send_sem=up_send.at[k, p], recv_sem=up_recv.at[k, p],
            device_id={"tile": lax.rem(t + 1, nt)}, device_id_type=MESH)
        dn = pltpu.make_async_remote_copy(
            src_ref=src, dst_ref=below.at[:, rows, :],
            send_sem=dn_send.at[k, p], recv_sem=dn_recv.at[k, p],
            device_id={"tile": lax.rem(t + nt - 1, nt)}, device_id_type=MESH)
        halos[k, p] = (up, dn, s)

        @pl.when(t < nt - 1)
        def _():
            up.start()

        @pl.when(t > 0)
        def _():
            dn.start()

    row16 = lax.broadcasted_iota(jnp.int32, (16, 128), 0)
    lane16 = lax.broadcasted_iota(jnp.int32, (16, 128), 1)

    def pick(row, lane):
        return jnp.where((row16 == row) & (lane16 == lane), 1.0, 0.0).astype(jnp.bfloat16)

    edges = [None]

    def send_edges():
        for d in range(nz):
            total_edge = jnp.zeros((16, fb), jnp.float32)
            for c in range(2):
                if d > 0:
                    total_edge += lax.dot_general(pick(2 * c, 127), x_ref[c, :, d * wb - 128:d * wb], NT,
                                                  preferred_element_type=jnp.float32)
                if d < nz - 1:
                    total_edge += lax.dot_general(pick(2 * c + 1, 0), x_ref[c, :, (d + 1) * wb:(d + 1) * wb + 128], NT,
                                                  preferred_element_type=jnp.float32)
            edge_out[d] = total_edge.astype(jnp.bfloat16)
        for k in range(1, nz):
            d = lax.rem(z + k, nz)
            copy = pltpu.make_async_remote_copy(
                src_ref=edge_out.at[d], dst_ref=edge_in.at[z],
                send_sem=edge_send.at[k], recv_sem=edge_recv.at[k],
                device_id={"frame": d}, device_id_type=MESH)
            copy.start()
            edges.append(copy)
        edge_in[z] = edge_out[z]

    for p in range(min(AHEAD, pieces)):
        send_piece(p)
        send_halo(0, p)
    for p in range(AHEAD, pieces):
        separate(p)
    send_edges()

    own = pltpu.make_async_copy(
        x_ref.at[:, :, own_cols], center.at[:, pl.ds(pl.multiple_of(z * fb, 16), fb), :], own_sem)
    own.start()
    own.wait()

    lane = lax.broadcasted_iota(jnp.int32, (16, wb), 1)
    outer_first, outer_last = (z == 0), (z == nz - 1)
    at_first, at_last = lane == 0, lane == wb - 1
    col_scale = jnp.where((at_first & outer_first) | (at_last & outer_last), 1.0, 0.5)
    row_scale = jnp.where((t == 0) | (t == nt - 1), 1.0, 0.5)
    eye = jnp.where(row16 == lane16, 1.0, 0.0).astype(jnp.bfloat16)

    def strain_piece(p):
        for k in range(nz):
            up, dn, s = halos[k, p]

            @pl.when(t > 0)
            def _(up=up):
                up.wait_recv()

            @pl.when(t < nt - 1)
            def _(dn=dn):
                dn.wait_recv()

            if p == 0:
                if k > 0:
                    edges[k].wait_recv()
                edge_cols[k] = lax.dot_general(edge_in[s], eye, TN, preferred_element_type=jnp.float32)

        def body(k, carry):
            at = frame_rows(lax.rem(z - k + nz, nz), p)
            cols = edge_cols[k, p * part:(p + 1) * part, :]

            @pl.when(t == 0)
            def _():
                above[:, at, :] = center[:, at, :]

            @pl.when(t == nt - 1)
            def _():
                below[:, at, :] = center[:, at, :]

            def column(f, c):
                before = jnp.where(at_first, jnp.where(outer_first, f, cols[:, 2 * c:2 * c + 1]), pltpu.roll(f, 1, 1))
                after = jnp.where(at_last, jnp.where(outer_last, f, cols[:, 2 * c + 1:2 * c + 2]),
                                  pltpu.roll(f, wb - 1, 1))
                return (after - before) * col_scale

            def row(c):
                return (below[c, at, :].astype(jnp.float32) - above[c, at, :].astype(jnp.float32)) * row_scale

            s_ref[0, at, :] = column(center[0, at, :].astype(jnp.float32), 0).astype(jnp.bfloat16)
            s_ref[1, at, :] = row(1).astype(jnp.bfloat16)
            s_ref[2, at, :] = (0.5 * (row(0) + column(center[1, at, :].astype(jnp.float32), 1))).astype(jnp.bfloat16)
            return carry

        lax.fori_loop(0, nz, body, 0)

    for p in range(pieces + 1):
        if p < pieces:
            for k in range(1, nz):
                blocks[k, p].wait_recv()
                send_halo(k, p)
            if p + AHEAD < pieces:
                send_piece(p + AHEAD)
                send_halo(0, p + AHEAD)
        if p > 0:
            strain_piece(p - 1)

    packed = [(i, j) for i in range(frames // BLOCK) for j in range(i + 1)]
    half = len(packed) // 2

    def products(which):
        mine = packed[which * half:(which + 1) * half]
        for j0 in range(0, frames // BLOCK, 2):
            inside = [(i, j) for i, j in mine if j0 <= j < j0 + 2]
            if not inside:
                continue
            i0, i1 = min(inside)[0], max(inside)[0] + 1
            value = jnp.zeros(((i1 - i0) * BLOCK, 2 * BLOCK), jnp.float32)
            for c in range(3):
                value += lax.dot_general(s_ref[c, i0 * BLOCK:i1 * BLOCK, :],
                                         s_ref[c, j0 * BLOCK:(j0 + 2) * BLOCK, :], NT,
                                         preferred_element_type=jnp.float32)
            for i, j in inside:
                index = packed.index((i, j))
                acc[index * BLOCK:(index + 1) * BLOCK, :] = value[
                    (i - i0) * BLOCK:(i - i0 + 1) * BLOCK, (j - j0) * BLOCK:(j - j0 + 1) * BLOCK]

    def on_core(which, half_index):
        @pl.when(core == which)
        def _():
            products(half_index)

    on_core(0, 1)
    on_core(1, 0)

    lo, place, slot, trail = 0, 0, 0, []
    for name, peers, size, split in stages:
        me = member(name, 0)[0]
        mine = pl.ds(pl.multiple_of(place + me * size, 8), size)
        copies = []
        for k in range(1, peers):
            _, index, device = member(name, k)
            give = lo + index * size if split else lo
            copy = pltpu.make_async_remote_copy(
                src_ref=acc.at[pl.ds(pl.multiple_of(give, 8), size), :], dst_ref=landing.at[mine, :],
                send_sem=sum_send.at[slot], recv_sem=sum_recv.at[slot],
                device_id=device, device_id_type=MESH)
            copy.start()
            copies.append(copy)
            slot += 1
        if name == "core":
            on_core(0, 0)
            on_core(1, 1)
        keep = lo + me * size if split else lo
        at = pl.ds(pl.multiple_of(keep, 8), size)
        landing[mine, :] = acc[at, :]
        for copy in copies:
            copy.wait()
        value = landing[place:place + size, :]
        for n in range(1, peers):
            value += landing[place + n * size:place + (n + 1) * size, :]
        acc[at, :] = value
        if split:
            trail.append((name, peers, size, keep))
        lo = keep
        place += peers * size
    at = pl.ds(pl.multiple_of(lo, 8), stages[-1][2])
    total[at, :] = acc[at, :]
    for name, peers, size, keep in reversed(trail):
        at = pl.ds(pl.multiple_of(keep, 8), size)
        copies = []
        for k in range(1, peers):
            copy = pltpu.make_async_remote_copy(
                src_ref=total.at[at, :], dst_ref=total.at[at, :],
                send_sem=sum_send.at[slot], recv_sem=sum_recv.at[slot],
                device_id=member(name, k)[2], device_id_type=MESH)
            copy.start()
            copies.append(copy)
            slot += 1
        for copy in copies:
            copy.wait()
    gram_ref[...] = total[...]

    for k in range(1, nz):
        edges[k].wait_send()
    for k in range(nz):
        for p in range(pieces):
            up, dn, _ = halos[k, p]
            if k > 0:
                blocks[k, p].wait_send()

            @pl.when(t < nt - 1)
            def _(up=up):
                up.wait_send()

            @pl.when(t > 0)
            def _(dn=dn):
                dn.wait_send()


def exchange(x, nz, nt):
    fb, width = x.shape[0], x.shape[2]
    wb, frames = width // nz, fb * nz
    nb, pieces = frames // BLOCK, fb // PIECE
    rows = nb * (nb + 1) // 2 * BLOCK
    stages = sum_stages(nz, nt, rows)
    landing = sum(stage[1] * stage[2] for stage in stages)
    steps = 2 * sum(stage[1] - 1 for stage in stages)
    dma = pltpu.SemaphoreType.DMA
    vmem = pl.BlockSpec(memory_space=pltpu.VMEM)
    return pl.pallas_call(
        functools.partial(exchange_kernel, nz, nt, stages),
        out_shape=(jax.ShapeDtypeStruct((rows, BLOCK), jnp.float32),
                   jax.ShapeDtypeStruct((3, frames, wb), jnp.bfloat16)),
        in_specs=[vmem],
        out_specs=(vmem, vmem),
        scratch_shapes=[
            pltpu.VMEM((2, fb, width), jnp.bfloat16),
            pltpu.VMEM((2, frames, wb), jnp.bfloat16),
            pltpu.VMEM((2, frames, wb), jnp.bfloat16),
            pltpu.VMEM((2, frames, wb), jnp.bfloat16),
            pltpu.VMEM((nz, 16, fb), jnp.bfloat16),
            pltpu.VMEM((nz, 16, fb), jnp.bfloat16),
            pltpu.VMEM((nz, fb, 128), jnp.float32),
            pltpu.VMEM((rows, BLOCK), jnp.float32),
            pltpu.VMEM((landing, BLOCK), jnp.float32),
            pltpu.VMEM((rows, BLOCK), jnp.float32),
            dma, dma((nz, pieces)), dma((nz, pieces)), dma((nz,)), dma((nz,)),
            dma((nz, pieces)), dma((nz, pieces)), dma((nz, pieces)), dma((nz, pieces)),
            dma((steps,)), dma((steps,)),
        ],
        compiler_params=pltpu.CompilerParams(
            collective_id=0, has_side_effects=True, vmem_limit_bytes=40 * 1024 * 1024),
    )(x)


def factor_block(a):
    n = a.shape[0]
    shape = (GROUP, n)
    row8 = lax.broadcasted_iota(jnp.int32, shape, 0)
    lane8 = lax.broadcasted_iota(jnp.int32, shape, 1)
    tiles = n // GROUP
    left = [a[GROUP * i:GROUP * (i + 1), :] for i in range(tiles)]
    right = [jnp.where(row8 + GROUP * i == lane8, 1.0, 0.0) for i in range(tiles)]

    def row_of(tile, p):
        return jnp.broadcast_to(tile[p:p + 1, :], shape)

    for g in range(tiles):
        first = GROUP * g
        columns = [jnp.broadcast_to(left[g][:, first + q:first + q + 1], shape) for q in range(GROUP)]
        entry = {(p, q): row_of(columns[q], p) for p in range(GROUP) for q in range(p + 1)}
        r = []
        for q in range(GROUP):
            r.append(lax.rsqrt(entry[q, q]))
            for p in range(q + 1, GROUP):
                entry[p, q] = entry[p, q] * r[q]
            for p in range(q + 1, GROUP):
                for m in range(q + 1, p + 1):
                    entry[p, m] = entry[p, m] - entry[p, q] * entry[m, q]
        tops = []
        for tile in (left[g], right[g]):
            rows = [row_of(tile, p) for p in range(GROUP)]
            for q in range(GROUP):
                rows[q] = rows[q] * r[q]
                for p in range(q + 1, GROUP):
                    rows[p] = rows[p] - entry[p, q] * rows[q]
            tops.append(rows)
        for i in range(g + 1, tiles):
            c = [jnp.broadcast_to(left[i][:, first + q:first + q + 1], shape) for q in range(GROUP)]
            for q in range(GROUP):
                c[q] = c[q] * r[q]
                for m in range(q + 1, GROUP):
                    c[m] = c[m] - c[q] * entry[m, q]
            for q in range(GROUP):
                left[i] = left[i] - c[q] * tops[0][q]
                right[i] = right[i] - c[q] * tops[1][q]
        packed = []
        for rows in tops:
            value = rows[0]
            for q in range(1, GROUP):
                value = jnp.where(row8 == q, rows[q], value)
            packed.append(value)
        left[g], right[g] = packed
    return jnp.concatenate(left, axis=0), jnp.concatenate(right, axis=0)


def basis_kernel(scale, g_ref, s_ref, basis_ref, factor_ref, work, planes, staged, out_sem):
    n = factor_ref.shape[0]
    wide = n // 2
    nb = n // BLOCK
    row = lax.broadcasted_iota(jnp.int32, (BLOCK, BLOCK), 0)
    col = lax.broadcasted_iota(jnp.int32, (BLOCK, BLOCK), 1)

    work[...] = jnp.zeros_like(work)
    index = 0
    for i in range(nb):
        for j in range(i + 1):
            block = g_ref[index * BLOCK:(index + 1) * BLOCK, :]
            work[j, :, i * BLOCK:(i + 1) * BLOCK] = block.T
            index += 1
        work[i, :, n + i * BLOCK:n + (i + 1) * BLOCK] = jnp.where(row == col, 1.0, 0.0)

    def step(k, carry):
        diag = pl.ds(pl.multiple_of(k * BLOCK, BLOCK), BLOCK)
        upper, inverse = factor_block(work[k, :, diag])
        window = pl.ds(pl.multiple_of(k * BLOCK, BLOCK), n + BLOCK)
        strip = jnp.dot(inverse, work[k, :, window], precision=EXACT, preferred_element_type=jnp.float32)
        work[k, :, window] = strip
        work[k, :, diag] = jnp.where(row <= col, upper, 0.0)
        for i in range(1, nb):
            @pl.when(i > k)
            def _(i=i):
                work[i, :, window] = work[i, :, window] - lax.dot_general(
                    work[k, :, i * BLOCK:(i + 1) * BLOCK], work[k, :, window], TN, precision=EXACT,
                    preferred_element_type=jnp.float32)
        return carry

    lax.fori_loop(0, nb, step, 0)

    for i in range(nb):
        for j in range(nb):
            at = slice(j * BLOCK, (j + 1) * BLOCK)
            block = work[i, :, at] * (1.0 / scale) if j >= i else jnp.zeros((BLOCK, BLOCK), jnp.float32)
            factor_ref[i * BLOCK:(i + 1) * BLOCK, at] = block
        m = work[i, :, n:2 * n] * scale
        head = m.astype(jnp.bfloat16)
        half, at = i * BLOCK // wide, (i * BLOCK) % wide
        planes[half, at:at + BLOCK, :] = head
        planes[half, wide + at:wide + at + BLOCK, :] = (m - head.astype(jnp.float32)).astype(jnp.bfloat16)
    for c in range(3):
        for i in range(n // wide):
            depth = (i + 1) * wide
            value = jnp.dot(planes[i, :, :depth], s_ref[c, :depth, :], preferred_element_type=jnp.float32)
            staged[c, i * wide:(i + 1) * wide, :] = (value[:wide] + value[wide:]).astype(jnp.bfloat16)
        pltpu.make_async_copy(staged.at[c], basis_ref.at[c], out_sem.at[c]).start()
    for c in range(3):
        pltpu.make_async_copy(staged.at[c], basis_ref.at[c], out_sem.at[c]).wait()


def orthonormal(gram, strain, scale):
    frames = strain.shape[1]
    nb = frames // BLOCK
    vmem = pl.BlockSpec(memory_space=pltpu.VMEM)
    return pl.pallas_call(
        functools.partial(basis_kernel, scale),
        out_shape=(jax.ShapeDtypeStruct(strain.shape, jnp.bfloat16),
                   jax.ShapeDtypeStruct((frames, frames), jnp.float32)),
        in_specs=[vmem, vmem],
        out_specs=(pl.BlockSpec(memory_space=pl.ANY), vmem),
        scratch_shapes=[
            pltpu.VMEM((nb, BLOCK, 2 * frames), jnp.float32),
            pltpu.VMEM((2, frames, frames), jnp.bfloat16),
            pltpu.VMEM(strain.shape, jnp.bfloat16),
            pltpu.SemaphoreType.DMA((3,)),
        ],
        compiler_params=pltpu.CompilerParams(vmem_limit_bytes=40 * 1024 * 1024),
    )(gram, strain)


def local(nz, nt, displacement):
    frames, rows, width = displacement.shape[0] * nz, displacement.shape[2] * nt, displacement.shape[3]
    scale = math.sqrt(3 * rows * width)
    x = displacement[:, :, 0, :]
    gram, strain = exchange(x, nz, nt)
    basis, factor = orthonormal(gram, strain, scale)
    return jnp.transpose(basis, (1, 0, 2))[:, :, None, :], factor


def solution(mesh):
    return jax.shard_map(
        functools.partial(local, mesh.shape["frame"], mesh.shape["tile"]),
        mesh=mesh,
        in_specs=(P("frame", None, "tile", None),),
        out_specs=(P(None, None, "tile", "frame"), P()),
        check_vma=False,
    )
```
